256 devices in a mesh: section: 2 (over core), dp: 4 (over y), latent: 32 (over z, x).
Axes of the slice: x: 4, y: 4, z: 8, core: 2. Of those that a mesh axis runs over, the one named last changes fastest.
Arguments:
- tokens: bfloat16 [512, 5120], P(None, 'dp'), may hold values from -8 to 8
- cotangent: bfloat16 [512, 5120], P(None, 'dp'), may hold values from -6 to 6
- enc_weight: bfloat16 [2, 5120, 32768], P('section', 'dp', 'latent'), may hold values from -0.078125 to 0.078125
- enc_bias: float32 [2, 32768], P('section', 'latent'), may hold values from -3 to 3
- dec_weight: bfloat16 [2, 32768, 5120], P('section', 'latent', 'dp'), may hold values from -0.078125 to 0.078125
- dec_bias: float32 [2, 5120], P('section', 'dp'), may hold values from -3 to 3
- ln_gain: float32 [2, 5120], P('section', 'dp'), may hold values from 0.1 to 1.9
- ln_bias: float32 [2, 5120], P('section', 'dp'), may hold values from -3 to 3
- in_weight: bfloat16 [2, 5120, 12288], P('section', 'dp', 'latent'), may hold values from -0.078125 to 0.078125
- in_bias: float32 [2, 12288], P('section', 'latent'), may hold values from -3 to 3
- out_weight: bfloat16 [2, 12288, 5120], P('section', 'latent', 'dp'), may hold values from -0.0546875 to 0.0546875
- out_bias: float32 [2, 5120], P('section', 'dp'), may hold values from -3 to 3
Outputs:
- latent_effect: bfloat16 [2, 512, 32768], P('section', 'dp', 'latent')
- error_effect: float32 [2, 512], P('section', 'dp')
The draws below stay inside these ranges and needn't reach their ends.
All inputs are finite; a program needn't handle non-finite values.
Results may differ from the reference program's by a relative error of at most 0.02.
Values may be sent and summed in bfloat16 or wider, within the bound.
No kernel may reach another device: no remote copies, remote signals or barrier semaphores. Data moves between devices by JAX's collectives and lax.ppermute only.
A program may use at most 128 MiB of HBM per device.

```python
import jax
import jax.numpy as jnp
from jax import lax

D = 5120
F = 32768
HID = 12288
TOKENS = 512


def draw_tokens(key, part):
    key = jax.random.fold_in(key, 11)
    column = jnp.arange(D, dtype=jnp.float32) / D
    first_key = jax.random.fold_in(key, 0)
    values = jax.random.normal(first_key, (TOKENS, D), jnp.float32) * (0.6 * 3.0 ** column)
    return jnp.clip(values, -8.0, 8.0).astype(jnp.bfloat16)


def steps_of(own_key, shape, shards, least, high):
    gain, own = 1.0, jax.random.fold_in(own_key, 6)
    for axis_at, blocks in shards:
        heights = jnp.exp(jax.random.uniform(jax.random.fold_in(own, axis_at), (blocks,), jnp.float32, least / len(shards), high / len(shards)))
        gain = gain * jnp.repeat(heights, shape[axis_at] // blocks).reshape([-1 if axis == axis_at else 1 for axis in range(len(shape))])
    return gain


def gaussian(own_key, extent, spread, reach, pieces=(), kind=jnp.bfloat16):
    drawn = jax.random.normal(own_key, extent, jnp.float32) * spread
    if len(pieces) > 0:
        drawn = steps_of(own_key, extent, pieces, -0.22, 0.18) * drawn
    return jnp.clip(drawn, min=-reach, max=reach).astype(kind)


def setup_inputs(seed: int = 0) -> dict:
    splits = jax.random.split(jax.random.key(seed), 13)
    tokens = draw_tokens(jax.random.fold_in(splits[12], 71), 0)
    cotangent = gaussian(splits[1], (TOKENS, D), 1.0, 6.0, ((1, 4),))
    enc_weight = gaussian(splits[2], (2, D, F), D ** -0.5, 0.078125, ((0, 2), (1, 4), (2, 32)))
    enc_bias = gaussian(splits[3], (2, F), 0.5, 3.0, ((0, 2), (1, 32)), jnp.float32)
    dec_weight = gaussian(splits[4], (2, F, D), D ** -0.5, 0.078125, ((0, 2), (1, 32), (2, 4)))
    dec_bias = gaussian(splits[5], (2, D), 0.5, 3.0, ((0, 2), (1, 4)), jnp.float32)
    ln_gain = jnp.clip(1.0 + 0.18 * jax.random.normal(splits[6], (2, D), jnp.float32), 0.1, 1.9)
    ln_bias = gaussian(splits[7], (2, D), 0.5, 3.0, ((0, 2), (1, 4)), jnp.float32)
    in_weight = gaussian(splits[8], (2, D, HID), D ** -0.5, 0.078125, ((0, 2), (1, 4), (2, 32)))
    in_bias = gaussian(splits[9], (2, HID), 0.5, 3.0, ((0, 2), (1, 32)), jnp.float32)
    out_weight = gaussian(splits[10], (2, HID, D), HID ** -0.5, 0.0546875, ((0, 2), (1, 32), (2, 4)))
    out_bias = gaussian(splits[11], (2, D), 0.5, 3.0, ((0, 2), (1, 4)), jnp.float32)
    return {"tokens": tokens, "cotangent": cotangent, "enc_weight": enc_weight, "enc_bias": enc_bias, "dec_weight": dec_weight, "dec_bias": dec_bias, "ln_gain": ln_gain, "ln_bias": ln_bias, "in_weight": in_weight, "in_bias": in_bias, "out_weight": out_weight, "out_bias": out_bias}


EPSILON = 1e-05
SQRT_HALF = 0.7071067811865476
INV_SQRT_TAU = 0.3989422804014327

def gelu_slope(values):
    cumulative = 0.5 * (1.0 + lax.erf(values * SQRT_HALF))
    return cumulative + values * jnp.exp(-0.5 * values * values) * INV_SQRT_TAU

def section_forward(residual, norm_gain, norm_shift, enc_w, enc_b, in_w, in_b, out_w, out_b):
    resid_f = residual.astype(jnp.float32)
    mean_row = lax.optimization_barrier(jnp.mean(resid_f, axis=-1, keepdims=True))
    square_row = lax.optimization_barrier(jnp.mean(resid_f * resid_f, axis=-1, keepdims=True))
    inv_std = lax.rsqrt(square_row - mean_row * mean_row + EPSILON)
    normed = (resid_f - mean_row) * inv_std
    ln_out = (normed * norm_gain + norm_shift).astype(jnp.bfloat16)
    pre_sum = jnp.dot(residual, enc_w, preferred_element_type=jnp.float32) + enc_b
    latent_codes = jnp.maximum(pre_sum, 0.0).astype(jnp.bfloat16)
    hidden = jnp.dot(ln_out, in_w, preferred_element_type=jnp.float32) + in_b
    act_out = jax.nn.gelu(hidden, approximate=False).astype(jnp.bfloat16)
    next_resid = (resid_f + jnp.dot(act_out, out_w, preferred_element_type=jnp.float32) + out_b).astype(jnp.bfloat16)
    return (next_resid, (resid_f, normed, inv_std, latent_codes, hidden))

def section_backward(saved_state, grad_out, norm_gain, in_w, out_w, dec_w, dec_b):
    resid_f, normed, inv_std, latent_codes, hidden = saved_state
    grad_act = jnp.dot(grad_out, out_w.T, preferred_element_type=jnp.float32)
    grad_hidden = (grad_act * gelu_slope(hidden)).astype(jnp.bfloat16)
    grad_ln = jnp.dot(grad_hidden, in_w.T, preferred_element_type=jnp.float32)
    grad_norm = grad_ln * norm_gain
    grad_resid = (grad_norm - lax.optimization_barrier(jnp.mean(grad_norm, axis=-1, keepdims=True)) - normed * lax.optimization_barrier(jnp.mean(grad_norm * normed, axis=-1, keepdims=True))) * inv_std
    grad_in = (grad_out.astype(jnp.float32) + grad_resid).astype(jnp.bfloat16)
    grad_codes = jnp.dot(grad_in, dec_w.T, preferred_element_type=jnp.float32)
    effect = (latent_codes.astype(jnp.float32) * grad_codes).astype(jnp.bfloat16)
    rebuilt = jnp.dot(latent_codes, dec_w, preferred_element_type=jnp.float32) + dec_b
    error_sum = lax.optimization_barrier(jnp.sum((resid_f - rebuilt) * grad_in.astype(jnp.float32), axis=-1))
    return (grad_in, effect, error_sum)

def reference(tokens, cotangent, enc_weight, enc_bias, dec_weight, dec_bias, ln_gain, ln_bias, in_weight, in_bias, out_weight, out_bias):
    residual = tokens
    saved_list = []
    for layer_index in range(2):
        residual, saved_state = section_forward(residual, ln_gain[layer_index], ln_bias[layer_index], enc_weight[layer_index], enc_bias[layer_index], in_weight[layer_index], in_bias[layer_index], out_weight[layer_index], out_bias[layer_index])
        saved_list.append(saved_state)
    gradient = cotangent
    effects = [None, None]
    errors = [None, None]
    for layer_index in (1, 0):
        gradient, effects[layer_index], errors[layer_index] = section_backward(saved_list[layer_index], gradient, ln_gain[layer_index], in_weight[layer_index], out_weight[layer_index], dec_weight[layer_index], dec_bias[layer_index])
    return (jnp.stack(effects), jnp.stack(errors))
```

```python
import jax
import jax.numpy as jnp
from jax import lax
from jax.sharding import PartitionSpec as P

D = 5120
EPSILON = 1e-05
SQRT_HALF = 0.7071067811865476
INV_SQRT_TAU = 0.3989422804014327
CONTRACT_LAST = (((1,), (1,)), ((), ()))
F32 = jnp.float32
BF16 = jnp.bfloat16


def gelu_slope(values):
    cumulative = 0.5 * (1.0 + lax.erf(values * SQRT_HALF))
    return cumulative + values * jnp.exp(-0.5 * values * values) * INV_SQRT_TAU


def split3(values):
    high = values.astype(BF16)
    rest = values - high.astype(F32)
    middle = rest.astype(BF16)
    low = (rest - middle.astype(F32)).astype(BF16)
    return [high, middle, low]


def dot(left, right):
    return jnp.dot(left, right, preferred_element_type=F32)


def dot_t(left, right):
    return lax.dot_general(left, right, CONTRACT_LAST, preferred_element_type=F32)


def spread(values, axis):
    count = lax.axis_size(axis)
    copies = jnp.broadcast_to(values[None], (count,) + values.shape)
    return lax.all_to_all(copies, axis, 0, 0)


def exchange(values, axis):
    count = lax.axis_size(axis)
    rows = values.shape[0] // count
    return lax.all_to_all(values.reshape(count, rows, values.shape[1]), axis, 0, 0)


def turn(values, axis, by):
    count = lax.axis_size(axis)
    return lax.ppermute(values, axis, [(i, (i + by) % count) for i in range(count)])


def gather_ring(values, axis):
    return [values] + [turn(values, axis, by) for by in range(1, lax.axis_size(axis))]


def total_ring(values, axis):
    return sum(part.astype(F32) for part in gather_ring(values, axis))


def scatter_ring(values, axis):
    count, place = lax.axis_size(axis), lax.axis_index(axis)
    rows = values.shape[0] // count

    def block(by):
        return lax.dynamic_slice_in_dim(values, (place + by) % count * rows, rows, 0)

    parts = [turn(block(by), axis, by) for by in range(1, count)]
    return block(0).astype(F32) + sum(part.astype(F32) for part in parts)


def pack_rows(values, width, rows):
    terms = jnp.stack(split3(values.reshape(-1, width))).reshape(-1, width)
    return jnp.pad(terms, ((0, rows - terms.shape[0]), (0, 0)))


def unpack_rows(terms, count):
    terms = terms[..., : 3 * count, :].astype(F32)
    return terms[..., :count, :] + terms[..., count : 2 * count, :] + terms[..., 2 * count :, :]


def on_device(
    tokens,
    cotangent,
    enc_weight,
    enc_bias,
    dec_weight,
    dec_bias,
    ln_gain,
    ln_bias,
    in_weight,
    in_bias,
    out_weight,
    out_bias,
):
    dp_count = lax.axis_size("dp")
    latent_count = lax.axis_size("latent")
    all_rows, width = tokens.shape
    half = all_rows // 2
    share = half // latent_count
    block = all_rows // dp_count
    hid = in_weight.shape[2]
    core = lax.axis_index("section")
    first = core == 0
    dp_place = lax.axis_index("dp")
    latent_place = lax.axis_index("latent")
    swap = [(0, 1), (1, 0)]

    def other(values):
        return lax.ppermute(values, "section", swap)

    def pick(mine_if_first, mine_if_second):
        return jnp.where(first, mine_if_first, mine_if_second)

    def own_rows(values):
        return lax.dynamic_slice_in_dim(values, latent_place * share, share, 0)

    in_w = in_weight[0]
    out_w = out_weight[0]
    gained = (in_w.astype(F32) * ln_gain[0][:, None]).astype(BF16)
    column_sum = jnp.sum(gained.astype(F32), axis=0)
    shift_in = jnp.sum(in_w.astype(F32) * ln_bias[0][:, None], axis=0)
    pad_bias = jnp.pad(out_bias[0], (0, -width % hid))
    vector_count = 3 + pad_bias.shape[0] // hid
    vectors = jnp.concatenate([column_sum, shift_in, in_bias[0], pad_bias])

    def row_parts(resid):
        resid_f = resid.astype(F32)
        local_mean = jnp.mean(resid_f, axis=1)
        centred = resid_f - local_mean[:, None]
        return local_mean, jnp.sum(centred * centred, axis=1)

    def stat_columns(local_mean, square):
        stats = jnp.stack(split3(local_mean) + split3(square), axis=1)
        return jnp.pad(stats, ((0, 0), (0, 128 - stats.shape[1])))

    def row_stats(parts):
        means, squares = [], []
        for stats in parts:
            stats = stats[:, :6].astype(F32)
            means.append(stats[:, 0] + stats[:, 1] + stats[:, 2])
            squares.append(stats[:, 3] + stats[:, 4] + stats[:, 5])
        mean = sum(means) / dp_count
        aparts = [local_mean - mean for local_mean in means]
        variance = sum(squares) / D + sum(apart * apart for apart in aparts) / dp_count
        return mean, lax.rsqrt(variance + EPSILON), aparts

    def pre_hidden(parts, aparts, inv, sums):
        total = sum(part.astype(F32) for part in parts)
        total = total + sum(apart[:, None] * s[None] for apart, s in zip(aparts, sums))
        return total * inv[:, None]

    tokens_half = lax.dynamic_slice_in_dim(tokens, core * half, half, 0)
    cot_half = lax.dynamic_slice_in_dim(cotangent, core * half, half, 0)
    mean_all, square_all = row_parts(tokens)
    forward_all = (dot(tokens, gained) - mean_all[:, None] * column_sum[None]).astype(BF16)
    grad_all = dot_t(cotangent, out_w).astype(BF16)
    packed = pack_rows(vectors, hid, 32)
    there = other(jnp.concatenate([pick(forward_all[half:], grad_all[:half]), packed], axis=0))
    part_0 = pick(forward_all[:half], there[:half])
    grad_act_part = pick(there[:half], grad_all[half:])
    vectors_there = unpack_rows(there[half:], vector_count)
    vectors = vectors.reshape(-1, hid)
    vectors_0 = pick(vectors, vectors_there)
    vectors_1 = pick(vectors_there, vectors)

    gained_there = other(gained)
    out_there = other(out_w)
    gained_0, gained_1 = pick(gained, gained_there), pick(gained_there, gained)
    out_w0 = pick(out_w, out_there)

    def gathered(part, stats, layer_vectors):
        rows = pack_rows(layer_vectors[:2].reshape(-1), hid, 16)
        payload = jnp.concatenate([part, rows], axis=0)
        stats = jnp.pad(stats, ((0, 16), (0, 0)))
        got = gather_ring(jnp.concatenate([payload, stats], axis=1), "dp")
        mean, inv, aparts = row_stats([g[:half, hid:] for g in got])
        dp_vectors = [unpack_rows(g[half:, :hid], 2) for g in got]
        sums = [v[0] for v in dp_vectors]
        pre = pre_hidden([g[:half, :hid] for g in got], aparts, inv, sums)
        shift = sum(v[1] for v in dp_vectors) + layer_vectors[2]
        return pre, pre + shift[None], mean, inv, sum(sums)

    def half_of(values):
        return lax.dynamic_slice_in_dim(values, core * half, half, 0)

    stats_0 = stat_columns(half_of(mean_all), half_of(square_all))
    pre_0, hidden_0, mean_0, inv_0, sums_0 = gathered(part_0, stats_0, vectors_0)
    act_0 = jax.nn.gelu(hidden_0, approximate=False).astype(BF16)
    mlp = exchange(dot(act_0, out_w0).astype(BF16), "latent")
    tokens_rows = own_rows(tokens_half).astype(F32)
    bias_row = vectors_0[3:].reshape(-1)[:width]
    resid_rows = (tokens_rows + jnp.sum(mlp.astype(F32), axis=0) + bias_row[None]).astype(BF16)
    resid_half = spread(resid_rows, "latent").reshape(half, width)

    local_mean, square = row_parts(resid_half)
    part_1 = dot(resid_half, gained_1) - local_mean[:, None] * vectors_1[0][None]
    pre_1, hidden_1, mean_1, inv_1, sums_1 = gathered(
        part_1.astype(BF16), stat_columns(local_mean, square), vectors_1
    )
    grad_act_1 = total_ring(grad_act_part, "dp")

    def backward(grad_act, hidden, pre, weight, sums, resid, mean, inv, grad_rows):
        grad_hidden = (grad_act * gelu_slope(hidden)).astype(BF16)
        grad_f = grad_hidden.astype(F32)
        total = jnp.sum(grad_f * sums[None], axis=1)
        cross = jnp.sum(grad_f * pre, axis=1)
        extra = jnp.stack(split3(total) + split3(cross), axis=1)
        extra = jnp.pad(extra, ((0, 0), (0, 128 - extra.shape[1])))
        partial = dot_t(grad_hidden, weight).astype(BF16)
        summed = exchange(jnp.concatenate([partial, extra], axis=1), "latent")
        summed = jnp.sum(summed.astype(F32), axis=0)
        grad_norm, extra = summed[:, :width], summed[:, width : width + 6] / D
        mean_grad = (extra[:, 0] + extra[:, 1] + extra[:, 2])[:, None]
        mean_cross = (extra[:, 3] + extra[:, 4] + extra[:, 5])[:, None]
        inv_rows = own_rows(inv)[:, None]
        normed = (resid - own_rows(mean)[:, None]) * inv_rows
        grad_resid = inv_rows * (grad_norm - mean_grad - normed * mean_cross)
        new_rows = (grad_rows + grad_resid).astype(BF16)
        return new_rows, spread(new_rows, "latent").reshape(half, width)

    cot_rows = own_rows(cot_half).astype(F32)
    grad_rows_1, grad_half_1 = backward(
        grad_act_1, hidden_1, pre_1, gained_1, sums_1, resid_rows.astype(F32), mean_1, inv_1, cot_rows
    )
    grad_act_0 = total_ring(dot_t(grad_half_1, out_w0).astype(BF16), "dp")
    _, grad_half_0 = backward(
        grad_act_0, hidden_0, pre_0, gained_0, sums_0, tokens_rows, mean_0, inv_0,
        grad_rows_1.astype(F32),
    )

    resid_all = pick(tokens, jnp.concatenate([other(resid_half), resid_half], axis=0))
    pre_codes = scatter_ring(dot(resid_all, enc_weight[0]).astype(BF16), "dp")
    codes = jnp.maximum(pre_codes + enc_bias[0][None], 0.0).astype(BF16)

    grad_there = other(pick(grad_half_1, grad_half_0))
    grad_all = pick(
        jnp.concatenate([grad_half_0, grad_there], axis=0),
        jnp.concatenate([grad_there, grad_half_1], axis=0),
    )
    effect = codes.astype(F32) * scatter_ring(dot_t(grad_all, dec_weight[0]).astype(BF16), "dp")
    error = (resid_all.astype(F32) - dec_bias[0][None]) * grad_all.astype(F32)
    error = (jnp.sum(error, axis=1) / latent_count).reshape(dp_count, 1, block)
    error = lax.all_to_all(error, "dp", 0, 0)
    error = jnp.sum(error, axis=0) - jnp.sum(effect, axis=1)[None]
    error = jnp.sum(spread(error, "latent"), axis=(0, 1))
    return effect.astype(BF16)[None], error[None]


def solution(mesh):
    in_specs = (
        P(None, "dp"),
        P(None, "dp"),
        P("section", "dp", "latent"),
        P("section", "latent"),
        P("section", "latent", "dp"),
        P("section", "dp"),
        P("section", "dp"),
        P("section", "dp"),
        P("section", "dp", "latent"),
        P("section", "latent"),
        P("section", "latent", "dp"),
        P("section", "dp"),
    )
    out_specs = (P("section", "dp", "latent"), P("section", "dp"))
    return jax.shard_map(
        on_device, mesh=mesh, in_specs=in_specs, out_specs=out_specs, check_vma=False
    )
```

```python
import jax
import jax.numpy as jnp
from jax import lax
from jax.experimental import pallas as pl
from jax.experimental.pallas import tpu as pltpu
from jax.sharding import PartitionSpec as P

D = 5120
EPSILON = 1e-05
SQRT_HALF = 0.7071067811865476
INV_SQRT_TAU = 0.3989422804014327
CONTRACT_LAST = (((1,), (1,)), ((), ()))
F32 = jnp.float32
BF16 = jnp.bfloat16


def gelu_slope(values):
    cumulative = 0.5 * (1.0 + lax.erf(values * SQRT_HALF))
    return cumulative + values * jnp.exp(-0.5 * values * values) * INV_SQRT_TAU


def split3(values):
    high = values.astype(BF16)
    rest = values - high.astype(F32)
    middle = rest.astype(BF16)
    low = (rest - middle.astype(F32)).astype(BF16)
    return [high, middle, low]


def dot(left, right):
    return jnp.dot(left, right, preferred_element_type=F32)


def dot_t(left, right):
    return lax.dot_general(left, right, CONTRACT_LAST, preferred_element_type=F32)


def spread(values, axis):
    count = lax.axis_size(axis)
    copies = jnp.broadcast_to(values[None], (count,) + values.shape)
    return lax.all_to_all(copies, axis, 0, 0)


def exchange(values, axis):
    count = lax.axis_size(axis)
    rows = values.shape[0] // count
    return lax.all_to_all(values.reshape(count, rows, values.shape[1]), axis, 0, 0)


def turn(values, axis, by):
    count = lax.axis_size(axis)
    return lax.ppermute(values, axis, [(i, (i + by) % count) for i in range(count)])


def gather_ring(values, axis):
    return [values] + [turn(values, axis, by) for by in range(1, lax.axis_size(axis))]


def total_ring(values, axis):
    return sum(part.astype(F32) for part in gather_ring(values, axis))


def scatter_ring(values, axis):
    count, place = lax.axis_size(axis), lax.axis_index(axis)
    rows = values.shape[0] // count

    def block(by):
        return lax.dynamic_slice_in_dim(values, (place + by) % count * rows, rows, 0)

    parts = [turn(block(by), axis, by) for by in range(1, count)]
    return block(0).astype(F32) + sum(part.astype(F32) for part in parts)


def start_kernel(
    core_ref,
    tokens_ref,
    cot_ref,
    in_w_ref,
    out_w_ref,
    gain_ref,
    bias_ref,
    in_bias_ref,
    out_bias_ref,
    gained_ref,
    mine_ref,
    send_ref,
):
    width, hid = in_w_ref.shape
    half = tokens_ref.shape[0] // 2
    gain = jnp.broadcast_to(gain_ref[...], (128, width)).T
    for at in range(0, hid, 128):
        columns = slice(at, at + 128)
        gained_ref[:, columns] = (in_w_ref[:, columns].astype(F32) * gain).astype(BF16)
    gained = gained_ref[...]
    column_sum = dot(jnp.ones((16, width), BF16), gained)[:1]
    terms = split3(bias_ref[...])
    terms = jnp.concatenate([t.astype(F32) for t in terms] + [jnp.zeros((13, width), F32)], axis=0)
    shift = jnp.sum(dot(terms.astype(BF16), in_w_ref[...]), axis=0, keepdims=True)
    rows = [column_sum, shift, in_bias_ref[...]]
    out_bias = out_bias_ref[...]
    for at in range(0, width, hid):
        piece = out_bias[:, at : at + hid]
        if piece.shape[1] < hid:
            piece = jnp.concatenate([piece, jnp.zeros((1, hid - piece.shape[1]), F32)], axis=1)
        rows.append(piece)
    rows.append(jnp.zeros((8 - len(rows), hid), F32))
    high = jnp.concatenate(rows, axis=0)
    packed = []
    for term in split3(high):
        packed.append(term.astype(F32))
    packed.append(jnp.zeros((8, hid), F32))
    packed = jnp.concatenate(packed, axis=0).astype(BF16)
    mine_ref[half : half + 32, :] = packed
    send_ref[half : half + 32, :] = packed

    @pl.when(core_ref[0] == 0)
    def _():
        for start, target in ((0, mine_ref), (half, send_ref)):
            rows = tokens_ref[start : start + half, :]
            mean = jnp.sum(rows.astype(F32), axis=1, keepdims=True) / width
            target[:half, :] = (dot(rows, gained) - mean * column_sum).astype(BF16)

    @pl.when(core_ref[0] != 0)
    def _():
        for start, target in ((half, mine_ref), (0, send_ref)):
            rows = cot_ref[start : start + half, :]
            target[:half, :] = dot_t(rows, out_w_ref[...]).astype(BF16)


def start_products(core, tokens, cotangent, in_w, out_w, gain, bias, in_bias, out_bias):
    width, hid = in_w.shape
    half = tokens.shape[0] // 2
    part = jax.ShapeDtypeStruct((half + 32, hid), BF16)
    return pl.pallas_call(
        start_kernel,
        out_shape=(jax.ShapeDtypeStruct((width, hid), BF16), part, part),
        in_specs=[pl.BlockSpec(memory_space=pltpu.SMEM)]
        + [pl.BlockSpec(memory_space=pltpu.VMEM)] * 8,
        out_specs=(pl.BlockSpec(memory_space=pltpu.VMEM),) * 3,
        compiler_params=pltpu.CompilerParams(vmem_limit_bytes=40 * 1024 * 1024),
        cost_estimate=pl.CostEstimate(
            flops=4 * half * width * hid, bytes_accessed=7_000_000, transcendentals=0
        ),
    )(core.reshape(1), tokens, cotangent, in_w, out_w, gain, bias, in_bias, out_bias)


def unpack_vectors(part, half):
    terms = part[..., half : half + 24, :].astype(F32)
    return terms[..., :8, :] + terms[..., 8:16, :] + terms[..., 16:24, :]


def on_device(
    tokens,
    cotangent,
    enc_weight,
    enc_bias,
    dec_weight,
    dec_bias,
    ln_gain,
    ln_bias,
    in_weight,
    in_bias,
    out_weight,
    out_bias,
):
    dp_count = lax.axis_size("dp")
    latent_count = lax.axis_size("latent")
    all_rows, width = tokens.shape
    half = all_rows // 2
    share = half // latent_count
    block = all_rows // dp_count
    hid = in_weight.shape[2]
    core = lax.axis_index("section")
    first = core == 0
    dp_place = lax.axis_index("dp")
    latent_place = lax.axis_index("latent")
    swap = [(0, 1), (1, 0)]

    def other(values):
        return lax.ppermute(values, "section", swap)

    def pick(mine_if_first, mine_if_second):
        return jnp.where(first, mine_if_first, mine_if_second)

    def own_rows(values):
        return lax.dynamic_slice_in_dim(values, latent_place * share, share, 0)

    in_w = in_weight[0]
    out_w = out_weight[0]

    def row_parts(resid):
        resid_f = resid.astype(F32)
        local_mean = jnp.mean(resid_f, axis=1)
        centred = resid_f - local_mean[:, None]
        return local_mean, jnp.sum(centred * centred, axis=1)

    def with_stats(part, local_mean, square):
        stats = jnp.stack(split3(local_mean) + split3(square))
        stats = stats.reshape(-1, hid)
        return part + jnp.pad(stats, ((half + 24, 8 - stats.shape[0]), (0, 0)))

    def row_stats(parts):
        means, squares = [], []
        for part in parts:
            count = 6 * half // hid
            stats = part[half + 24 : half + 24 + count].reshape(6, half).astype(F32)
            means.append(stats[0] + stats[1] + stats[2])
            squares.append(stats[3] + stats[4] + stats[5])
        mean = sum(means) / dp_count
        aparts = [local_mean - mean for local_mean in means]
        variance = sum(squares) / D + sum(apart * apart for apart in aparts) / dp_count
        return mean, lax.rsqrt(variance + EPSILON), aparts

    gained, mine, send = start_products(
        core, tokens, cotangent, in_w, out_w, ln_gain, ln_bias, in_bias, out_bias
    )
    there = other(send)
    tokens_half = lax.dynamic_slice_in_dim(tokens, core * half, half, 0)
    cot_half = lax.dynamic_slice_in_dim(cotangent, core * half, half, 0)
    part_0 = with_stats(pick(mine, there), *row_parts(tokens_half))
    part_grad = pick(there, mine)
    vectors_0 = unpack_vectors(part_0, half)
    vectors_1 = unpack_vectors(part_grad, half)
    gained_there = other(gained)
    gained_0, gained_1 = pick(gained, gained_there), pick(gained_there, gained)
    out_w0 = pick(out_w, other(out_w))

    def gathered(part, in_b):
        got = gather_ring(part, "dp")
        mean, inv, aparts = row_stats(got)
        vectors = [unpack_vectors(g, half) for g in got]
        sums = [v[0] for v in vectors]
        total = sum(g[:half].astype(F32) for g in got)
        total = total + sum(apart[:, None] * s[None] for apart, s in zip(aparts, sums))
        pre = total * inv[:, None]
        shift = sum(v[1] for v in vectors) + in_b
        return pre, pre + shift[None], mean, inv, sum(sums)

    pre_0, hidden_0, mean_0, inv_0, sums_0 = gathered(part_0, vectors_0[2])
    act_0 = jax.nn.gelu(hidden_0, approximate=False).astype(BF16)
    mlp = exchange(dot(act_0, out_w0).astype(BF16), "latent")
    tokens_rows = own_rows(tokens_half).astype(F32)
    bias_row = vectors_0[3:7].reshape(-1)[:width]
    resid_rows = (tokens_rows + jnp.sum(mlp.astype(F32), axis=0) + bias_row[None]).astype(BF16)
    grad_act_1 = total_ring(part_grad[:half], "dp")
    resid_rows, grad_act_1 = lax.optimization_barrier((resid_rows, grad_act_1))
    resid_half = spread(resid_rows, "latent").reshape(half, width)

    local_mean, square = row_parts(resid_half)
    part_1 = dot(resid_half, gained_1) - local_mean[:, None] * vectors_1[0][None]
    part_1 = jnp.concatenate([part_1.astype(BF16), part_grad[half:]], axis=0)
    resid_there = other(resid_half)
    pre_1, hidden_1, mean_1, inv_1, sums_1 = gathered(
        with_stats(part_1, local_mean, square), vectors_1[2]
    )
    hidden_1, resid_there = lax.optimization_barrier((hidden_1, resid_there))

    def backward(grad_act, hidden, pre, weight, sums, resid, mean, inv, grad_rows):
        grad_hidden = (grad_act * gelu_slope(hidden)).astype(BF16)
        grad_f = grad_hidden.astype(F32)
        total = jnp.sum(grad_f * sums[None], axis=1)
        cross = jnp.sum(grad_f * pre, axis=1)
        extra = jnp.stack(split3(total) + split3(cross), axis=1)
        extra = jnp.pad(extra, ((0, 0), (0, 128 - extra.shape[1])))
        partial = dot_t(grad_hidden, weight).astype(BF16)
        summed = exchange(jnp.concatenate([partial, extra], axis=1), "latent")
        summed = jnp.sum(summed.astype(F32), axis=0)
        grad_norm, extra = summed[:, :width], summed[:, width : width + 6] / D
        mean_grad = (extra[:, 0] + extra[:, 1] + extra[:, 2])[:, None]
        mean_cross = (extra[:, 3] + extra[:, 4] + extra[:, 5])[:, None]
        inv_rows = own_rows(inv)[:, None]
        normed = (resid - own_rows(mean)[:, None]) * inv_rows
        grad_resid = inv_rows * (grad_norm - mean_grad - normed * mean_cross)
        new_rows = (grad_rows + grad_resid).astype(BF16)
        return new_rows, spread(new_rows, "latent").reshape(half, width)

    cot_rows = own_rows(cot_half).astype(F32)
    grad_rows_1, grad_half_1 = backward(
        grad_act_1, hidden_1, pre_1, gained_1, sums_1, resid_rows.astype(F32), mean_1, inv_1, cot_rows
    )
    resid_all = pick(tokens, jnp.concatenate([resid_there, resid_half], axis=0))
    pre_codes = scatter_ring(dot(resid_all, enc_weight[0]).astype(BF16), "dp")
    grad_half_1, pre_codes = lax.optimization_barrier((grad_half_1, pre_codes))
    grad_act_0 = total_ring(dot_t(grad_half_1, out_w0).astype(BF16), "dp")
    _, grad_half_0 = backward(
        grad_act_0, hidden_0, pre_0, gained_0, sums_0, tokens_rows, mean_0, inv_0,
        grad_rows_1.astype(F32),
    )

    codes = jnp.maximum(pre_codes + enc_bias[0][None], 0.0).astype(BF16)
    resid_own = lax.dynamic_slice_in_dim(resid_all, core * half, half, 0)
    resid_rest = lax.dynamic_slice_in_dim(resid_all, (1 - core) * half, half, 0)

    def attributed(grad, resid):
        error = (resid.astype(F32) - dec_bias[0][None]) * grad.astype(F32)
        error = jnp.stack(split3(jnp.sum(error, axis=1) / latent_count), axis=1)
        error = jnp.pad(error, ((0, 0), (0, 128 - error.shape[1])))
        return jnp.concatenate([dot_t(grad, dec_weight[0]).astype(BF16), error], axis=1)

    rest = attributed(other(pick(grad_half_1, grad_half_0)), resid_rest)
    own = attributed(pick(grad_half_0, grad_half_1), resid_own)
    parts = pick(jnp.concatenate([own, rest], axis=0), jnp.concatenate([rest, own], axis=0))
    summed = scatter_ring(parts, "dp")
    latents = codes.shape[1]
    effect = codes.astype(F32) * summed[:, :latents]
    error = jnp.sum(summed[:, latents : latents + 3], axis=1) - jnp.sum(effect, axis=1)
    error = jnp.sum(spread(error[None], "latent"), axis=(0, 1))
    return effect.astype(BF16)[None], error[None]


def solution(mesh):
    in_specs = (
        P(None, "dp"),
        P(None, "dp"),
        P("section", "dp", "latent"),
        P("section", "latent"),
        P("section", "latent", "dp"),
        P("section", "dp"),
        P("section", "dp"),
        P("section", "dp"),
        P("section", "dp", "latent"),
        P("section", "latent"),
        P("section", "latent", "dp"),
        P("section", "dp"),
    )
    out_specs = (P("section", "dp", "latent"), P("section", "dp"))
    return jax.shard_map(
        on_device, mesh=mesh, in_specs=in_specs, out_specs=out_specs, check_vma=False
    )
```

```python
import jax
import jax.numpy as jnp
from jax import lax
from jax.experimental import pallas as pl
from jax.experimental.pallas import tpu as pltpu
from jax.sharding import PartitionSpec as P

D = 5120
EPSILON = 1e-05
SQRT_HALF = 0.7071067811865476
INV_SQRT_TAU = 0.3989422804014327
CONTRACT_LAST = (((1,), (1,)), ((), ()))
F32 = jnp.float32
BF16 = jnp.bfloat16


def gelu_slope(values):
    cumulative = 0.5 * (1.0 + lax.erf(values * SQRT_HALF))
    return cumulative + values * jnp.exp(-0.5 * values * values) * INV_SQRT_TAU


def split3(values):
    high = values.astype(BF16)
    rest = values - high.astype(F32)
    middle = rest.astype(BF16)
    low = (rest - middle.astype(F32)).astype(BF16)
    return [high, middle, low]


def dot(left, right):
    return jnp.dot(left, right, preferred_element_type=F32)


def dot_t(left, right):
    return lax.dot_general(left, right, CONTRACT_LAST, preferred_element_type=F32)


def spread(values, axis):
    count = lax.axis_size(axis)
    copies = jnp.broadcast_to(values[None], (count,) + values.shape)
    return lax.all_to_all(copies, axis, 0, 0)


def exchange(values, axis):
    count = lax.axis_size(axis)
    rows = values.shape[0] // count
    return lax.all_to_all(values.reshape(count, rows, values.shape[1]), axis, 0, 0)


def turn(values, axis, by):
    count = lax.axis_size(axis)
    return lax.ppermute(values, axis, [(i, (i + by) % count) for i in range(count)])


def gather_ring(values, axis):
    return [values] + [turn(values, axis, by) for by in range(1, lax.axis_size(axis))]


def total_ring(values, axis):
    return sum(part.astype(F32) for part in gather_ring(values, axis))


def scatter_ring(values, axis):
    count, place = lax.axis_size(axis), lax.axis_index(axis)
    rows = values.shape[0] // count

    def block(by):
        return lax.dynamic_slice_in_dim(values, (place + by) % count * rows, rows, 0)

    parts = [turn(block(by), axis, by) for by in range(1, count)]
    return block(0).astype(F32) + sum(part.astype(F32) for part in parts)


def start_kernel(
    tokens_hbm,
    cot_hbm,
    in_w_hbm,
    out_w_hbm,
    gain_hbm,
    bias_hbm,
    in_bias_hbm,
    out_bias_hbm,
    gained_ref,
    mine_ref,
    send_ref,
    tokens_ref,
    cot_ref,
    in_w_ref,
    out_w_ref,
    gain_ref,
    bias_ref,
    in_bias_ref,
    out_bias_ref,
    sems,
):
    width, hid = in_w_ref.shape
    half = tokens_ref.shape[0] // 2
    first = lax.axis_index("section") == 0
    pairs = (
        (gain_hbm, gain_ref),
        (in_w_hbm, in_w_ref),
        (bias_hbm, bias_ref),
        (in_bias_hbm, in_bias_ref),
        (out_bias_hbm, out_bias_ref),
        (tokens_hbm, tokens_ref),
        (cot_hbm, cot_ref),
        (out_w_hbm, out_w_ref),
    )
    copies = [pltpu.make_async_copy(a, b, sems.at[k]) for k, (a, b) in enumerate(pairs)]
    for copy in copies:
        copy.start()
    for copy in copies[:5]:
        copy.wait()
    gain = jnp.broadcast_to(gain_ref[...], (128, width)).T
    for at in range(0, hid, 128):
        columns = slice(at, at + 128)
        gained_ref[:, columns] = (in_w_ref[:, columns].astype(F32) * gain).astype(BF16)
    gained = gained_ref[...]
    column_sum = dot(jnp.ones((16, width), BF16), gained)[:1]
    terms = split3(bias_ref[...])
    terms = jnp.concatenate([t.astype(F32) for t in terms] + [jnp.zeros((13, width), F32)], axis=0)
    shift = jnp.sum(dot(terms.astype(BF16), in_w_ref[...]), axis=0, keepdims=True)
    rows = [column_sum, shift, in_bias_ref[...]]
    out_bias = out_bias_ref[...]
    for at in range(0, width, hid):
        piece = out_bias[:, at : at + hid]
        if piece.shape[1] < hid:
            piece = jnp.concatenate([piece, jnp.zeros((1, hid - piece.shape[1]), F32)], axis=1)
        rows.append(piece)
    rows.append(jnp.zeros((8 - len(rows), hid), F32))
    high = jnp.concatenate(rows, axis=0)
    packed = []
    for term in split3(high):
        packed.append(term.astype(F32))
    packed.append(jnp.zeros((8, hid), F32))
    packed = jnp.concatenate(packed, axis=0).astype(BF16)
    mine_ref[half : half + 32, :] = packed
    send_ref[half : half + 32, :] = packed

    for copy in copies[5:]:
        copy.wait()

    @pl.when(first)
    def _():
        for start, target in ((0, mine_ref), (half, send_ref)):
            rows = tokens_ref[start : start + half, :]
            mean = jnp.sum(rows.astype(F32), axis=1, keepdims=True) / width
            target[:half, :] = (dot(rows, gained) - mean * column_sum).astype(BF16)

    @pl.when(jnp.logical_not(first))
    def _():
        for start, target in ((half, mine_ref), (0, send_ref)):
            rows = cot_ref[start : start + half, :]
            target[:half, :] = dot_t(rows, out_w_ref[...]).astype(BF16)


def in_vmem(kernel, out_shape, *args, flops=0):
    return pl.pallas_call(
        kernel,
        out_shape=out_shape,
        in_specs=[pl.BlockSpec(memory_space=pltpu.VMEM)] * len(args),
        out_specs=tuple(pl.BlockSpec(memory_space=pltpu.VMEM) for _ in out_shape),
        compiler_params=pltpu.CompilerParams(vmem_limit_bytes=32 * 1024 * 1024),
        cost_estimate=pl.CostEstimate(flops=flops, bytes_accessed=4_000_000, transcendentals=0),
    )(*args)


def start_products(*args):
    tokens, _, in_w = args[:3]
    width, hid = in_w.shape
    half = tokens.shape[0] // 2
    part = jax.ShapeDtypeStruct((half + 32, hid), BF16)
    return pl.pallas_call(
        start_kernel,
        out_shape=(jax.ShapeDtypeStruct((width, hid), BF16), part, part),
        in_specs=[pl.BlockSpec(memory_space=pl.ANY)] * len(args),
        out_specs=(pl.BlockSpec(memory_space=pltpu.VMEM),) * 3,
        scratch_shapes=[pltpu.VMEM(arg.shape, arg.dtype) for arg in args]
        + [pltpu.SemaphoreType.DMA((len(args),))],
        compiler_params=pltpu.CompilerParams(vmem_limit_bytes=40 * 1024 * 1024),
        cost_estimate=pl.CostEstimate(
            flops=4 * half * width * hid, bytes_accessed=7_000_000, transcendentals=0
        ),
    )(*args)


def read_hidden(parts):
    half = parts[0].shape[0] - 32
    lower = [part[half : half + 32, :].astype(F32) for part in parts]
    vectors = [low[:8] + low[8:16] + low[16:24] for low in lower]
    means = [(low[24:25] + low[25:26] + low[26:27])[:, :half] for low in lower]
    squares = [(low[27:28] + low[28:29] + low[29:30])[:, :half] for low in lower]
    count = len(parts)
    mean = sum(means) / count
    aparts = [local_mean - mean for local_mean in means]
    variance = sum(squares) / D + sum(apart * apart for apart in aparts) / count
    rows = [lax.rsqrt(variance + EPSILON), mean] + aparts
    rows.append(jnp.zeros((128 - len(rows), half), F32))
    columns = jnp.concatenate(rows, axis=0).T
    total = parts[0][:half, :].astype(F32)
    for part in parts[1:]:
        total = total + part[:half, :].astype(F32)
    for place, vector in enumerate(vectors):
        total = total + columns[:, 2 + place : 3 + place] * vector[:1]
    pre = total * columns[:, :1]
    summed = sum(vectors)
    return pre, pre + (summed[1:2] + vectors[0][2:3]), columns, summed


def forward_kernel(*refs):
    parts, (out_w_ref, y_ref, pre_ref, hidden_ref, columns_ref, sums_ref) = refs[:-6], refs[-6:]
    pre, hidden, columns, sums = read_hidden(parts)
    pre_ref[...] = pre
    hidden_ref[...] = hidden
    columns_ref[...] = columns
    sums_ref[...] = sums
    act = 0.5 * hidden * (1.0 + lax.erf(hidden * SQRT_HALF))
    y_ref[...] = dot(act.astype(BF16), out_w_ref[...]).astype(BF16)


def write_grad(grad_act, hidden, pre, sums, weight, y_ref):
    width = weight.shape[0]
    grad_hidden = (grad_act * gelu_slope(hidden)).astype(BF16)
    grad_f = grad_hidden.astype(F32)
    total = jnp.sum(grad_f * sums, axis=1, keepdims=True)
    cross = jnp.sum(grad_f * pre, axis=1, keepdims=True)
    lane = lax.broadcasted_iota(jnp.int32, (grad_f.shape[0], 128), 1)
    extra = jnp.zeros(lane.shape, F32)
    for index, term in enumerate(split3(total) + split3(cross)):
        extra = jnp.where(lane == index, term.astype(F32), extra)
    y_ref[:, :width] = dot_t(grad_hidden, weight).astype(BF16)
    y_ref[:, width:] = extra.astype(BF16)


def turn_kernel(*refs):
    parts, (grad_act_ref, weight_ref, y_ref, columns_ref) = refs[:-4], refs[-4:]
    pre, hidden, columns, sums = read_hidden(parts)
    columns_ref[...] = columns
    write_grad(grad_act_ref[...], hidden, pre, sums[:1], weight_ref[...], y_ref)


def backward_kernel(*refs):
    parts, (hidden_ref, pre_ref, sums_ref, weight_ref, y_ref) = refs[:-5], refs[-5:]
    grad_act = parts[0][...].astype(F32)
    for part in parts[1:]:
        grad_act = grad_act + part[...].astype(F32)
    write_grad(grad_act, hidden_ref[...], pre_ref[...], sums_ref[:1, :], weight_ref[...], y_ref)


def unpack_vectors(part, half):
    terms = part[..., half : half + 24, :].astype(F32)
    return terms[..., :8, :] + terms[..., 8:16, :] + terms[..., 16:24, :]


def on_device(
    tokens,
    cotangent,
    enc_weight,
    enc_bias,
    dec_weight,
    dec_bias,
    ln_gain,
    ln_bias,
    in_weight,
    in_bias,
    out_weight,
    out_bias,
):
    dp_count = lax.axis_size("dp")
    latent_count = lax.axis_size("latent")
    all_rows, width = tokens.shape
    half = all_rows // 2
    share = half // latent_count
    block = all_rows // dp_count
    hid = in_weight.shape[2]
    core = lax.axis_index("section")
    first = core == 0
    dp_place = lax.axis_index("dp")
    latent_place = lax.axis_index("latent")
    swap = [(0, 1), (1, 0)]

    def other(values):
        return lax.ppermute(values, "section", swap)

    def pick(mine_if_first, mine_if_second):
        return jnp.where(first, mine_if_first, mine_if_second)

    def own_rows(values):
        return lax.dynamic_slice_in_dim(values, latent_place * share, share, 0)

    in_w = in_weight[0]
    out_w = out_weight[0]

    def row_parts(resid):
        resid_f = resid.astype(F32)
        local_mean = jnp.mean(resid_f, axis=1)
        centred = resid_f - local_mean[:, None]
        return local_mean, jnp.sum(centred * centred, axis=1)

    def with_stats(part, local_mean, square):
        stats = jnp.stack(split3(local_mean) + split3(square))
        return part + jnp.pad(stats, ((half + 24, 2), (0, hid - half)))

    part_shape = jax.ShapeDtypeStruct((half, hid), F32)
    columns_shape = jax.ShapeDtypeStruct((half, 128), F32)
    y_shape = jax.ShapeDtypeStruct((half, width), BF16)
    grad_shape = jax.ShapeDtypeStruct((half, width + 128), BF16)
    flops = 2 * half * hid * width

    gained, mine, send = start_products(
        tokens, cotangent, in_w, out_w, ln_gain, ln_bias, in_bias, out_bias
    )
    there = other(send)
    tokens_half = lax.dynamic_slice_in_dim(tokens, core * half, half, 0)
    cot_half = lax.dynamic_slice_in_dim(cotangent, core * half, half, 0)
    part_0 = with_stats(pick(mine, there), *row_parts(tokens_half))
    part_grad = pick(there, mine)
    vectors_0 = unpack_vectors(part_0, half)
    vectors_1 = unpack_vectors(part_grad, half)
    gained_there = other(gained)
    gained_0, gained_1 = pick(gained, gained_there), pick(gained_there, gained)
    out_w0 = pick(out_w, other(out_w))

    y_0, pre_0, hidden_0, columns_0, sums_0 = in_vmem(
        forward_kernel,
        (y_shape, part_shape, part_shape, columns_shape, jax.ShapeDtypeStruct((8, hid), F32)),
        *gather_ring(part_0, "dp"),
        out_w0,
        flops=flops,
    )
    mlp = exchange(y_0, "latent")
    tokens_rows = own_rows(tokens_half).astype(F32)
    bias_row = vectors_0[3:7].reshape(-1)[:width]
    resid_rows = (tokens_rows + jnp.sum(mlp.astype(F32), axis=0) + bias_row[None]).astype(BF16)
    grad_act_1 = total_ring(part_grad[:half], "dp")
    resid_rows, grad_act_1 = lax.optimization_barrier((resid_rows, grad_act_1))
    resid_half = spread(resid_rows, "latent").reshape(half, width)

    local_mean, square = row_parts(resid_half)
    part_1 = dot(resid_half, gained_1) - local_mean[:, None] * vectors_1[0][None]
    part_1 = jnp.concatenate([part_1.astype(BF16), part_grad[half:]], axis=0)
    resid_there = other(resid_half)
    parts_1 = gather_ring(with_stats(part_1, local_mean, square), "dp")
    parts_1, resid_there = lax.optimization_barrier((parts_1, resid_there))

    def norm_grad(y, columns, resid, grad_rows):
        summed = jnp.sum(exchange(y, "latent").astype(F32), axis=0)
        grad_norm, extra = summed[:, :width], summed[:, width : width + 6] / D
        mean_grad = (extra[:, 0] + extra[:, 1] + extra[:, 2])[:, None]
        mean_cross = (extra[:, 3] + extra[:, 4] + extra[:, 5])[:, None]
        columns = own_rows(columns)
        inv, mean = columns[:, :1], columns[:, 1:2]
        normed = (resid - mean) * inv
        grad_resid = inv * (grad_norm - mean_grad - normed * mean_cross)
        new_rows = (grad_rows + grad_resid).astype(BF16)
        return new_rows, spread(new_rows, "latent").reshape(half, width)

    y_1, columns_1 = in_vmem(
        turn_kernel, (grad_shape, columns_shape), *parts_1, grad_act_1, gained_1, flops=flops
    )
    cot_rows = own_rows(cot_half).astype(F32)
    grad_rows_1, grad_half_1 = norm_grad(y_1, columns_1, resid_rows.astype(F32), cot_rows)
    resid_all = pick(tokens, jnp.concatenate([resid_there, resid_half], axis=0))
    pre_codes = scatter_ring(dot(resid_all, enc_weight[0]).astype(BF16), "dp")
    grad_half_1, pre_codes = lax.optimization_barrier((grad_half_1, pre_codes))
    parts_0 = gather_ring(dot_t(grad_half_1, out_w0).astype(BF16), "dp")
    (y_2,) = in_vmem(
        backward_kernel, (grad_shape,), *parts_0, hidden_0, pre_0, sums_0, gained_0, flops=flops
    )
    _, grad_half_0 = norm_grad(y_2, columns_0, tokens_rows, grad_rows_1.astype(F32))

    codes = jnp.maximum(pre_codes + enc_bias[0][None], 0.0).astype(BF16)
    resid_own = lax.dynamic_slice_in_dim(resid_all, core * half, half, 0)
    resid_rest = lax.dynamic_slice_in_dim(resid_all, (1 - core) * half, half, 0)

    def attributed(grad, resid):
        error = (resid.astype(F32) - dec_bias[0][None]) * grad.astype(F32)
        error = jnp.stack(split3(jnp.sum(error, axis=1) / latent_count), axis=1)
        error = jnp.pad(error, ((0, 0), (0, 128 - error.shape[1])))
        return jnp.concatenate([dot_t(grad, dec_weight[0]).astype(BF16), error], axis=1)

    rest = attributed(other(pick(grad_half_1, grad_half_0)), resid_rest)
    own = attributed(pick(grad_half_0, grad_half_1), resid_own)
    parts = pick(jnp.concatenate([own, rest], axis=0), jnp.concatenate([rest, own], axis=0))
    summed = scatter_ring(parts, "dp")
    latents = codes.shape[1]
    effect = codes.astype(F32) * summed[:, :latents]
    error = jnp.sum(summed[:, latents : latents + 3], axis=1) - jnp.sum(effect, axis=1)
    error = jnp.sum(spread(error[None], "latent"), axis=(0, 1))
    return effect.astype(BF16)[None], error[None]


def solution(mesh):
    in_specs = (
        P(None, "dp"),
        P(None, "dp"),
        P("section", "dp", "latent"),
        P("section", "latent"),
        P("section", "latent", "dp"),
        P("section", "dp"),
        P("section", "dp"),
        P("section", "dp"),
        P("section", "dp", "latent"),
        P("section", "latent"),
        P("section", "latent", "dp"),
        P("section", "dp"),
    )
    out_specs = (P("section", "dp", "latent"), P("section", "dp"))
    return jax.shard_map(
        on_device, mesh=mesh, in_specs=in_specs, out_specs=out_specs, check_vma=False
    )
```

```python
import jax
import jax.numpy as jnp
from jax import lax
from jax.experimental import pallas as pl
from jax.experimental.pallas import tpu as pltpu
from jax.sharding import PartitionSpec as P

D = 5120
EPSILON = 1e-05
SQRT_HALF = 0.7071067811865476
INV_SQRT_TAU = 0.3989422804014327
CONTRACT_LAST = (((1,), (1,)), ((), ()))
F32 = jnp.float32
BF16 = jnp.bfloat16


def gelu_slope(values):
    cumulative = 0.5 * (1.0 + lax.erf(values * SQRT_HALF))
    return cumulative + values * jnp.exp(-0.5 * values * values) * INV_SQRT_TAU


def split3(values):
    high = values.astype(BF16)
    rest = values - high.astype(F32)
    middle = rest.astype(BF16)
    low = (rest - middle.astype(F32)).astype(BF16)
    return [high, middle, low]


def dot(left, right):
    return jnp.dot(left, right, preferred_element_type=F32)


def dot_t(left, right):
    return lax.dot_general(left, right, CONTRACT_LAST, preferred_element_type=F32)


def spread(values, axis):
    count = lax.axis_size(axis)
    copies = jnp.broadcast_to(values[None], (count,) + values.shape)
    return lax.all_to_all(copies, axis, 0, 0)


def exchange(values, axis):
    count = lax.axis_size(axis)
    rows = values.shape[0] // count
    return lax.all_to_all(values.reshape(count, rows, values.shape[1]), axis, 0, 0)


def turn(values, axis, by):
    count = lax.axis_size(axis)
    return lax.ppermute(values, axis, [(i, (i + by) % count) for i in range(count)])


def gather_ring(values, axis):
    return [values] + [turn(values, axis, by) for by in range(1, lax.axis_size(axis))]


def total_ring(values, axis):
    return sum(part.astype(F32) for part in gather_ring(values, axis))


def scatter_ring(values, axis):
    count, place = lax.axis_size(axis), lax.axis_index(axis)
    rows = values.shape[0] // count

    def block(by):
        return lax.dynamic_slice_in_dim(values, (place + by) % count * rows, rows, 0)

    parts = [turn(block(by), axis, by) for by in range(1, count)]
    return block(0).astype(F32) + sum(part.astype(F32) for part in parts)


def start_kernel(
    tokens_hbm,
    cot_hbm,
    in_w_hbm,
    out_w_hbm,
    gain_hbm,
    bias_hbm,
    in_bias_hbm,
    out_bias_hbm,
    gained_ref,
    mine_ref,
    send_ref,
    tokens_ref,
    cot_ref,
    in_w_ref,
    out_w_ref,
    gain_ref,
    bias_ref,
    in_bias_ref,
    out_bias_ref,
    sems,
):
    width, hid = in_w_ref.shape
    half = tokens_ref.shape[0] // 2
    first = lax.axis_index("section") == 0
    pairs = (
        (gain_hbm, gain_ref),
        (in_w_hbm, in_w_ref),
        (bias_hbm, bias_ref),
        (in_bias_hbm, in_bias_ref),
        (out_bias_hbm, out_bias_ref),
        (tokens_hbm, tokens_ref),
        (cot_hbm, cot_ref),
        (out_w_hbm, out_w_ref),
    )
    copies = [pltpu.make_async_copy(a, b, sems.at[k]) for k, (a, b) in enumerate(pairs)]
    for copy in copies:
        copy.start()
    for copy in copies[:5]:
        copy.wait()
    gain = jnp.broadcast_to(gain_ref[...], (128, width)).T
    for at in range(0, hid, 128):
        columns = slice(at, at + 128)
        gained_ref[:, columns] = (in_w_ref[:, columns].astype(F32) * gain).astype(BF16)
    gained = gained_ref[...]
    column_sum = dot(jnp.ones((16, width), BF16), gained)[:1]
    terms = split3(bias_ref[...])
    terms = jnp.concatenate([t.astype(F32) for t in terms] + [jnp.zeros((13, width), F32)], axis=0)
    shift = jnp.sum(dot(terms.astype(BF16), in_w_ref[...]), axis=0, keepdims=True)
    rows = [column_sum, shift, in_bias_ref[...]]
    out_bias = out_bias_ref[...]
    for at in range(0, width, hid):
        piece = out_bias[:, at : at + hid]
        if piece.shape[1] < hid:
            piece = jnp.concatenate([piece, jnp.zeros((1, hid - piece.shape[1]), F32)], axis=1)
        rows.append(piece)
    rows.append(jnp.zeros((8 - len(rows), hid), F32))
    high = jnp.concatenate(rows, axis=0)
    packed = []
    for term in split3(high):
        packed.append(term.astype(F32))
    packed.append(jnp.zeros((8, hid), F32))
    packed = jnp.concatenate(packed, axis=0).astype(BF16)
    mine_ref[half : half + 32, :] = packed
    send_ref[half : half + 32, :] = packed

    for copy in copies[5:]:
        copy.wait()

    @pl.when(first)
    def _():
        for start, target in ((0, mine_ref), (half, send_ref)):
            rows = tokens_ref[start : start + half, :]
            mean = jnp.sum(rows.astype(F32), axis=1, keepdims=True) / width
            target[:half, :] = (dot(rows, gained) - mean * column_sum).astype(BF16)

    @pl.when(jnp.logical_not(first))
    def _():
        for start, target in ((half, mine_ref), (0, send_ref)):
            rows = cot_ref[start : start + half, :]
            target[:half, :] = dot_t(rows, out_w_ref[...]).astype(BF16)


def in_vmem(kernel, out_shape, *args, flops=0, scratch=()):
    return pl.pallas_call(
        kernel,
        out_shape=out_shape,
        in_specs=[pl.BlockSpec(memory_space=pltpu.VMEM)] * len(args),
        out_specs=tuple(pl.BlockSpec(memory_space=pltpu.VMEM) for _ in out_shape),
        scratch_shapes=scratch,
        compiler_params=pltpu.CompilerParams(vmem_limit_bytes=32 * 1024 * 1024),
        cost_estimate=pl.CostEstimate(flops=flops, bytes_accessed=4_000_000, transcendentals=0),
    )(*args)


def start_products(*args):
    tokens, _, in_w = args[:3]
    width, hid = in_w.shape
    half = tokens.shape[0] // 2
    part = jax.ShapeDtypeStruct((half + 32, hid), BF16)
    return pl.pallas_call(
        start_kernel,
        out_shape=(jax.ShapeDtypeStruct((width, hid), BF16), part, part),
        in_specs=[pl.BlockSpec(memory_space=pltpu.HBM)] * len(args),
        out_specs=(pl.BlockSpec(memory_space=pltpu.VMEM),) * 3,
        scratch_shapes=[pltpu.VMEM(arg.shape, arg.dtype) for arg in args]
        + [pltpu.SemaphoreType.DMA((len(args),))],
        compiler_params=pltpu.CompilerParams(vmem_limit_bytes=40 * 1024 * 1024),
        cost_estimate=pl.CostEstimate(
            flops=4 * half * width * hid, bytes_accessed=7_000_000, transcendentals=0
        ),
    )(*args)


def read_hidden(parts):
    half = parts[0].shape[0] - 32
    lower = [part[half : half + 32, :].astype(F32) for part in parts]
    vectors = [low[:8] + low[8:16] + low[16:24] for low in lower]
    means = [(low[24:25] + low[25:26] + low[26:27])[:, :half] for low in lower]
    squares = [(low[27:28] + low[28:29] + low[29:30])[:, :half] for low in lower]
    count = len(parts)
    mean = sum(means) / count
    aparts = [local_mean - mean for local_mean in means]
    variance = sum(squares) / D + sum(apart * apart for apart in aparts) / count
    rows = [lax.rsqrt(variance + EPSILON), mean] + aparts
    rows.append(jnp.zeros((128 - len(rows), half), F32))
    columns = jnp.concatenate(rows, axis=0).T
    total = parts[0][:half, :].astype(F32)
    for part in parts[1:]:
        total = total + part[:half, :].astype(F32)
    for place, vector in enumerate(vectors):
        total = total + columns[:, 2 + place : 3 + place] * vector[:1]
    pre = total * columns[:, :1]
    summed = sum(vectors)
    return pre, pre + (summed[1:2] + vectors[0][2:3]), columns, summed


def forward_kernel(*refs):
    parts, (out_w_ref, y_ref, pre_ref, hidden_ref, columns_ref, sums_ref) = refs[:-6], refs[-6:]
    pre, hidden, columns, sums = read_hidden(parts)
    pre_ref[...] = pre
    hidden_ref[...] = hidden
    columns_ref[...] = columns
    sums_ref[...] = sums
    act = 0.5 * hidden * (1.0 + lax.erf(hidden * SQRT_HALF))
    y_ref[...] = dot(act.astype(BF16), out_w_ref[...]).astype(BF16)


def write_grad(grad_act, hidden, pre, sums, weight, y_ref):
    width = weight.shape[0]
    grad_hidden = (grad_act * gelu_slope(hidden)).astype(BF16)
    grad_f = grad_hidden.astype(F32)
    total = jnp.sum(grad_f * sums, axis=1, keepdims=True)
    cross = jnp.sum(grad_f * pre, axis=1, keepdims=True)
    extra = columns_of(split3(total) + split3(cross), grad_f.shape[0])
    y_ref[:, :width] = dot_t(grad_hidden, weight).astype(BF16)
    y_ref[:, width:] = extra.astype(BF16)


def turn_kernel(*refs):
    parts, (grad_act_ref, weight_ref, y_ref, columns_ref) = refs[:-4], refs[-4:]
    pre, hidden, columns, sums = read_hidden(parts)
    columns_ref[...] = columns
    write_grad(grad_act_ref[...], hidden, pre, sums[:1], weight_ref[...], y_ref)


def backward_kernel(*refs):
    parts, (hidden_ref, pre_ref, sums_ref, weight_ref, y_ref) = refs[:-5], refs[-5:]
    grad_act = parts[0][...].astype(F32)
    for part in parts[1:]:
        grad_act = grad_act + part[...].astype(F32)
    write_grad(grad_act, hidden_ref[...], pre_ref[...], sums_ref[:1, :], weight_ref[...], y_ref)


def columns_of(terms, rows):
    lane = lax.broadcasted_iota(jnp.int32, (rows, 128), 1)
    columns = jnp.zeros(lane.shape, F32)
    for index, term in enumerate(terms):
        columns = jnp.where(lane == index, term.astype(F32), columns)
    return columns


def expand_kernel(resid_ref, weight_ref, below_ref, part_ref):
    half, width = resid_ref.shape
    hid = weight_ref.shape[1]
    resid = resid_ref[...]
    resid_f = resid.astype(F32)
    mean = jnp.sum(resid_f, axis=1, keepdims=True) / width
    centred = resid_f - mean
    square = jnp.sum(centred * centred, axis=1, keepdims=True)
    low = below_ref[half : half + 32, :].astype(F32)
    column_sum = low[:1] + low[8:9] + low[16:17]
    part_ref[:half, :] = (dot(resid, weight_ref[...]) - mean * column_sum).astype(BF16)
    stats = columns_of(split3(mean) + split3(square), half).T[:8]
    stats = jnp.concatenate([stats, jnp.zeros((8, hid - half), F32)], axis=1)
    part_ref[half : half + 32, :] = jnp.concatenate([low[:24], stats], axis=0).astype(BF16)


def write_copies(rows, rows_ref, copies_ref):
    rows_ref[...] = rows
    for place in range(copies_ref.shape[0]):
        copies_ref[place] = rows


def total_of(y_ref):
    total = y_ref[0].astype(F32)
    for place in range(1, y_ref.shape[0]):
        total = total + y_ref[place].astype(F32)
    return total


def share_kernel(y_ref, resid_ref, bias_ref, rows_ref, copies_ref):
    rows = resid_ref[...] + total_of(y_ref) + bias_ref[...]
    write_copies(rows.astype(BF16), rows_ref, copies_ref)


def norm_kernel(y_ref, columns_ref, resid_ref, grad_ref, rows_ref, copies_ref):
    width = resid_ref.shape[1]
    summed = total_of(y_ref)
    grad_norm, extra = summed[:, :width], summed[:, width:] / D
    mean_grad = extra[:, :1] + extra[:, 1:2] + extra[:, 2:3]
    mean_cross = extra[:, 3:4] + extra[:, 4:5] + extra[:, 5:6]
    inv, mean = columns_ref[:, :1], columns_ref[:, 1:2]
    normed = (resid_ref[...] - mean) * inv
    grad_resid = inv * (grad_norm - mean_grad - normed * mean_cross)
    write_copies((grad_ref[...] + grad_resid).astype(BF16), rows_ref, copies_ref)


def effect_kernel(own_ref, rest_ref, resid_ref, weight_ref, bias_ref, *refs):
    outs, grads_ref = refs[:-1], refs[-1]
    half = own_ref.shape[0]
    core, place = lax.axis_index("section"), lax.axis_index("dp")
    grads_ref[pl.ds(pl.multiple_of(core * half, half), half), :] = own_ref[...]
    grads_ref[pl.ds(pl.multiple_of((1 - core) * half, half), half), :] = rest_ref[...]
    latents = weight_ref.shape[0]
    block = outs[0].shape[0]
    for by, out in enumerate(outs):
        start = pl.multiple_of(lax.rem(place + by, len(outs)) * block, block)
        grad = grads_ref[pl.ds(start, block), :]
        out[:, :latents] = dot_t(grad, weight_ref[...]).astype(BF16)
        resid = resid_ref[pl.ds(start, block), :].astype(F32)
        error = (resid - bias_ref[...]) * grad.astype(F32)
        error = jnp.sum(error, axis=1, keepdims=True) / lax.axis_size("latent")
        out[:, latents:] = columns_of(split3(error), block).astype(BF16)


def unpack_vectors(part, half):
    terms = part[..., half : half + 24, :].astype(F32)
    return terms[..., :8, :] + terms[..., 8:16, :] + terms[..., 16:24, :]


def on_device(
    tokens,
    cotangent,
    enc_weight,
    enc_bias,
    dec_weight,
    dec_bias,
    ln_gain,
    ln_bias,
    in_weight,
    in_bias,
    out_weight,
    out_bias,
):
    dp_count = lax.axis_size("dp")
    latent_count = lax.axis_size("latent")
    all_rows, width = tokens.shape
    half = all_rows // 2
    share = half // latent_count
    block = all_rows // dp_count
    hid = in_weight.shape[2]
    core = lax.axis_index("section")
    first = core == 0
    dp_place = lax.axis_index("dp")
    latent_place = lax.axis_index("latent")
    swap = [(0, 1), (1, 0)]

    def other(values):
        return lax.ppermute(values, "section", swap)

    def pick(mine_if_first, mine_if_second):
        return jnp.where(first, mine_if_first, mine_if_second)

    def own_rows(values):
        return lax.dynamic_slice_in_dim(values, latent_place * share, share, 0)

    in_w = in_weight[0]
    out_w = out_weight[0]

    def row_parts(resid):
        resid_f = resid.astype(F32)
        local_mean = jnp.mean(resid_f, axis=1)
        centred = resid_f - local_mean[:, None]
        return local_mean, jnp.sum(centred * centred, axis=1)

    def with_stats(part, local_mean, square):
        stats = jnp.stack(split3(local_mean) + split3(square))
        return part + jnp.pad(stats, ((half + 24, 2), (0, hid - half)))

    part_shape = jax.ShapeDtypeStruct((half, hid), F32)
    columns_shape = jax.ShapeDtypeStruct((half, 128), F32)
    y_shape = jax.ShapeDtypeStruct((half, width), BF16)
    grad_shape = jax.ShapeDtypeStruct((half, width + 128), BF16)
    flops = 2 * half * hid * width

    gained, mine, send = start_products(
        tokens, cotangent, in_w, out_w, ln_gain, ln_bias, in_bias, out_bias
    )
    there = other(send)
    tokens_half = lax.dynamic_slice_in_dim(tokens, core * half, half, 0)
    cot_half = lax.dynamic_slice_in_dim(cotangent, core * half, half, 0)
    part_0 = with_stats(pick(mine, there), *row_parts(tokens_half))
    part_grad = pick(there, mine)
    vectors_0 = unpack_vectors(part_0, half)
    vectors_1 = unpack_vectors(part_grad, half)
    gained_there = other(gained)
    gained_0, gained_1 = pick(gained, gained_there), pick(gained_there, gained)
    out_w0 = pick(out_w, other(out_w))

    y_0, pre_0, hidden_0, columns_0, sums_0 = in_vmem(
        forward_kernel,
        (y_shape, part_shape, part_shape, columns_shape, jax.ShapeDtypeStruct((8, hid), F32)),
        *gather_ring(part_0, "dp"),
        out_w0,
        flops=flops,
    )
    tokens_rows = own_rows(tokens_half).astype(F32)
    bias_row = vectors_0[3:7].reshape(1, -1)[:, :width]
    row_shapes = (
        jax.ShapeDtypeStruct((share, width), BF16),
        jax.ShapeDtypeStruct((latent_count, share, width), BF16),
    )
    resid_rows, copies = in_vmem(
        share_kernel, row_shapes, exchange(y_0, "latent"), tokens_rows, bias_row
    )
    grad_act_1 = total_ring(part_grad[:half], "dp")
    copies, grad_act_1 = lax.optimization_barrier((copies, grad_act_1))
    resid_half = lax.all_to_all(copies, "latent", 0, 0).reshape(half, width)

    (part_1,) = in_vmem(
        expand_kernel,
        (jax.ShapeDtypeStruct((half + 32, hid), BF16),),
        resid_half,
        gained_1,
        part_grad,
        flops=flops,
    )
    resid_there = other(resid_half)
    parts_1 = gather_ring(part_1, "dp")
    parts_1, resid_there = lax.optimization_barrier((parts_1, resid_there))

    def norm_grad(y, columns, resid, grad_rows):
        rows, copies = in_vmem(
            norm_kernel, row_shapes, exchange(y, "latent"), own_rows(columns), resid, grad_rows
        )
        return rows, lax.all_to_all(copies, "latent", 0, 0).reshape(half, width)

    y_1, columns_1 = in_vmem(
        turn_kernel, (grad_shape, columns_shape), *parts_1, grad_act_1, gained_1, flops=flops
    )
    cot_rows = own_rows(cot_half).astype(F32)
    grad_rows_1, grad_half_1 = norm_grad(y_1, columns_1, resid_rows.astype(F32), cot_rows)
    resid_all = pick(tokens, jnp.concatenate([resid_there, resid_half], axis=0))
    pre_codes = scatter_ring(dot(resid_all, enc_weight[0]).astype(BF16), "dp")
    grad_half_1, pre_codes = lax.optimization_barrier((grad_half_1, pre_codes))
    parts_0 = gather_ring(dot_t(grad_half_1, out_w0).astype(BF16), "dp")
    (y_2,) = in_vmem(
        backward_kernel, (grad_shape,), *parts_0, hidden_0, pre_0, sums_0, gained_0, flops=flops
    )
    _, grad_half_0 = norm_grad(y_2, columns_0, tokens_rows, grad_rows_1.astype(F32))

    codes = jnp.maximum(pre_codes + enc_bias[0][None], 0.0).astype(BF16)
    parts = in_vmem(
        effect_kernel,
        (jax.ShapeDtypeStruct((block, codes.shape[1] + 128), BF16),) * dp_count,
        pick(grad_half_0, grad_half_1),
        other(pick(grad_half_1, grad_half_0)),
        resid_all,
        dec_weight[0],
        dec_bias,
        flops=2 * all_rows * width * codes.shape[1],
        scratch=[pltpu.VMEM((all_rows, width), BF16)],
    )
    summed = parts[0].astype(F32) + sum(
        turn(parts[by], "dp", by).astype(F32) for by in range(1, dp_count)
    )
    latents = codes.shape[1]
    effect = codes.astype(F32) * summed[:, :latents]
    error = jnp.sum(summed[:, latents : latents + 3], axis=1) - jnp.sum(effect, axis=1)
    error = jnp.sum(spread(error[None], "latent"), axis=(0, 1))
    return effect.astype(BF16)[None], error[None]


def solution(mesh):
    in_specs = (
        P(None, "dp"),
        P(None, "dp"),
        P("section", "dp", "latent"),
        P("section", "latent"),
        P("section", "latent", "dp"),
        P("section", "dp"),
        P("section", "dp"),
        P("section", "dp"),
        P("section", "dp", "latent"),
        P("section", "latent"),
        P("section", "latent", "dp"),
        P("section", "dp"),
    )
    out_specs = (P("section", "dp", "latent"), P("section", "dp"))
    return jax.shard_map(
        on_device, mesh=mesh, in_specs=in_specs, out_specs=out_specs, check_vma=False
    )
```

```python
import jax
import jax.numpy as jnp
from jax import lax
from jax.experimental import pallas as pl
from jax.experimental.pallas import tpu as pltpu
from jax.sharding import PartitionSpec as P

D = 5120
EPSILON = 1e-05
SQRT_HALF = 0.7071067811865476
INV_SQRT_TAU = 0.3989422804014327
CONTRACT_LAST = (((1,), (1,)), ((), ()))
F32 = jnp.float32
BF16 = jnp.bfloat16


def gelu_slope(values):
    cumulative = 0.5 * (1.0 + lax.erf(values * SQRT_HALF))
    return cumulative + values * jnp.exp(-0.5 * values * values) * INV_SQRT_TAU


def split3(values):
    high = values.astype(BF16)
    rest = values - high.astype(F32)
    middle = rest.astype(BF16)
    low = (rest - middle.astype(F32)).astype(BF16)
    return [high, middle, low]


def dot(left, right):
    return jnp.dot(left, right, preferred_element_type=F32)


def dot_t(left, right):
    return lax.dot_general(left, right, CONTRACT_LAST, preferred_element_type=F32)


def spread(values, axis):
    count = lax.axis_size(axis)
    copies = jnp.broadcast_to(values[None], (count,) + values.shape)
    return lax.all_to_all(copies, axis, 0, 0)


def exchange(values, axis):
    count = lax.axis_size(axis)
    rows = values.shape[0] // count
    return lax.all_to_all(values.reshape(count, rows, values.shape[1]), axis, 0, 0)


def turn(values, axis, by):
    count = lax.axis_size(axis)
    return lax.ppermute(values, axis, [(i, (i + by) % count) for i in range(count)])


def gather_ring(values, axis):
    return [values] + [turn(values, axis, by) for by in range(1, lax.axis_size(axis))]


def total_ring(values, axis):
    return sum(part.astype(F32) for part in gather_ring(values, axis))


def scatter_ring(values, axis):
    count, place = lax.axis_size(axis), lax.axis_index(axis)
    rows = values.shape[0] // count

    def block(by):
        return lax.dynamic_slice_in_dim(values, (place + by) % count * rows, rows, 0)

    parts = [turn(block(by), axis, by) for by in range(1, count)]
    return block(0).astype(F32) + sum(part.astype(F32) for part in parts)


def start_kernel(
    tokens_hbm,
    cot_hbm,
    in_w_hbm,
    out_w_hbm,
    gain_hbm,
    bias_hbm,
    in_bias_hbm,
    out_bias_hbm,
    gained_ref,
    mine_ref,
    send_ref,
    tokens_ref,
    cot_ref,
    in_w_ref,
    out_w_ref,
    gain_ref,
    bias_ref,
    in_bias_ref,
    out_bias_ref,
    sems,
):
    width, hid = in_w_ref.shape
    half = tokens_ref.shape[0] // 2
    first = lax.axis_index("section") == 0
    pairs = (
        (gain_hbm, gain_ref),
        (in_w_hbm, in_w_ref),
        (bias_hbm, bias_ref),
        (in_bias_hbm, in_bias_ref),
        (out_bias_hbm, out_bias_ref),
        (tokens_hbm, tokens_ref),
        (cot_hbm, cot_ref),
        (out_w_hbm, out_w_ref),
    )
    copies = [pltpu.make_async_copy(a, b, sems.at[k]) for k, (a, b) in enumerate(pairs)]
    for copy in copies:
        copy.start()
    for copy in copies[:5]:
        copy.wait()
    gain = jnp.broadcast_to(gain_ref[...], (128, width)).T
    for at in range(0, hid, 128):
        columns = slice(at, at + 128)
        gained_ref[:, columns] = (in_w_ref[:, columns].astype(F32) * gain).astype(BF16)
    gained = gained_ref[...]
    column_sum = dot(jnp.ones((16, width), BF16), gained)[:1]
    terms = split3(bias_ref[...])
    terms = jnp.concatenate([t.astype(F32) for t in terms] + [jnp.zeros((13, width), F32)], axis=0)
    shift = jnp.sum(dot(terms.astype(BF16), in_w_ref[...]), axis=0, keepdims=True)
    rows = [column_sum, shift, in_bias_ref[...]]
    out_bias = out_bias_ref[...]
    for at in range(0, width, hid):
        piece = out_bias[:, at : at + hid]
        if piece.shape[1] < hid:
            piece = jnp.concatenate([piece, jnp.zeros((1, hid - piece.shape[1]), F32)], axis=1)
        rows.append(piece)
    rows.append(jnp.zeros((8 - len(rows), hid), F32))
    high = jnp.concatenate(rows, axis=0)
    packed = []
    for term in split3(high):
        packed.append(term.astype(F32))
    packed.append(jnp.zeros((8, hid), F32))
    packed = jnp.concatenate(packed, axis=0).astype(BF16)
    mine_ref[half : half + 32, :] = packed
    send_ref[half : half + 32, :] = packed

    for copy in copies[5:]:
        copy.wait()

    @pl.when(first)
    def _():
        for start, target in ((0, mine_ref), (half, send_ref)):
            rows = tokens_ref[start : start + half, :]
            mean = jnp.sum(rows.astype(F32), axis=1, keepdims=True) / width
            target[:half, :] = (dot(rows, gained) - mean * column_sum).astype(BF16)

    @pl.when(jnp.logical_not(first))
    def _():
        for start, target in ((half, mine_ref), (0, send_ref)):
            rows = cot_ref[start : start + half, :]
            target[:half, :] = dot_t(rows, out_w_ref[...]).astype(BF16)


def in_vmem(kernel, out_shape, *args, flops=0, scratch=()):
    return pl.pallas_call(
        kernel,
        out_shape=out_shape,
        in_specs=[pl.BlockSpec(memory_space=pltpu.VMEM)] * len(args),
        out_specs=tuple(pl.BlockSpec(memory_space=pltpu.VMEM) for _ in out_shape),
        scratch_shapes=scratch,
        compiler_params=pltpu.CompilerParams(vmem_limit_bytes=14 * 1024 * 1024),
        cost_estimate=pl.CostEstimate(flops=flops, bytes_accessed=4_000_000, transcendentals=0),
    )(*args)


def start_products(*args):
    tokens, _, in_w = args[:3]
    width, hid = in_w.shape
    half = tokens.shape[0] // 2
    part = jax.ShapeDtypeStruct((half + 32, hid), BF16)
    return pl.pallas_call(
        start_kernel,
        out_shape=(jax.ShapeDtypeStruct((width, hid), BF16), part, part),
        in_specs=[pl.BlockSpec(memory_space=pl.ANY)] * len(args),
        out_specs=(pl.BlockSpec(memory_space=pltpu.VMEM),) * 3,
        scratch_shapes=[pltpu.VMEM(arg.shape, arg.dtype) for arg in args]
        + [pltpu.SemaphoreType.DMA((len(args),))],
        compiler_params=pltpu.CompilerParams(vmem_limit_bytes=58 * 1024 * 1024),
        cost_estimate=pl.CostEstimate(
            flops=4 * half * width * hid, bytes_accessed=7_000_000, transcendentals=0
        ),
    )(*args)


def read_hidden(parts):
    half = parts[0].shape[0] - 32
    lower = [part[half : half + 32, :].astype(F32) for part in parts]
    vectors = [low[:8] + low[8:16] + low[16:24] for low in lower]
    means = [(low[24:25] + low[25:26] + low[26:27])[:, :half] for low in lower]
    squares = [(low[27:28] + low[28:29] + low[29:30])[:, :half] for low in lower]
    count = len(parts)
    mean = sum(means) / count
    aparts = [local_mean - mean for local_mean in means]
    variance = sum(squares) / D + sum(apart * apart for apart in aparts) / count
    rows = [lax.rsqrt(variance + EPSILON), mean] + aparts
    rows.append(jnp.zeros((128 - len(rows), half), F32))
    columns = jnp.concatenate(rows, axis=0).T
    total = parts[0][:half, :].astype(F32)
    for part in parts[1:]:
        total = total + part[:half, :].astype(F32)
    for place, vector in enumerate(vectors):
        total = total + columns[:, 2 + place : 3 + place] * vector[:1]
    pre = total * columns[:, :1]
    summed = sum(vectors)
    shift = summed[1:2] + vectors[0][2:3]
    return pre, shift, columns, summed


def forward_kernel(*refs):
    parts, (out_w_ref, y_ref, state_ref) = refs[:-3], refs[-3:]
    pre, shift, columns, sums = read_hidden(parts)
    hidden = pre + shift
    half, hid = pre.shape
    state_ref[:half, :hid] = pre
    state_ref[:half, hid:] = columns
    state_ref[half : half + 8, :hid] = jnp.concatenate([sums[:1], shift, sums[2:]], axis=0)
    act = 0.5 * hidden * (1.0 + lax.erf(hidden * SQRT_HALF))
    y_ref[...] = dot(act.astype(BF16), out_w_ref[...]).astype(BF16)


def write_grad(grad_act, hidden, pre, sums, weight, y_ref):
    width = weight.shape[0]
    grad_hidden = (grad_act * gelu_slope(hidden)).astype(BF16)
    grad_f = grad_hidden.astype(F32)
    total = jnp.sum(grad_f * sums, axis=1, keepdims=True)
    cross = jnp.sum(grad_f * pre, axis=1, keepdims=True)
    extra = columns_of(split3(total) + split3(cross), grad_f.shape[0])
    y_ref[:, :width] = dot_t(grad_hidden, weight).astype(BF16)
    y_ref[:, width:] = extra.astype(BF16)


def turn_kernel(*refs):
    parts, (grad_act_ref, weight_ref, y_ref, columns_ref) = refs[:-4], refs[-4:]
    pre, shift, columns, sums = read_hidden(parts)
    columns_ref[...] = columns
    write_grad(grad_act_ref[...], pre + shift, pre, sums[:1], weight_ref[...], y_ref)


def backward_kernel(*refs):
    parts, (state_ref, weight_ref, y_ref) = refs[:-3], refs[-3:]
    half, hid = parts[0].shape
    grad_act = parts[0][...].astype(F32)
    for part in parts[1:]:
        grad_act = grad_act + part[...].astype(F32)
    pre, vectors = state_ref[:half, :hid], state_ref[half : half + 8, :hid]
    write_grad(grad_act, pre + vectors[1:2], pre, vectors[:1], weight_ref[...], y_ref)


def columns_of(terms, rows):
    lane = lax.broadcasted_iota(jnp.int32, (rows, 128), 1)
    columns = jnp.zeros(lane.shape, F32)
    for index, term in enumerate(terms):
        columns = jnp.where(lane == index, term.astype(F32), columns)
    return columns


def expand_kernel(resid_ref, weight_ref, below_ref, part_ref):
    half, width = resid_ref.shape
    hid = weight_ref.shape[1]
    resid = resid_ref[...]
    resid_f = resid.astype(F32)
    mean = jnp.sum(resid_f, axis=1, keepdims=True) / width
    centred = resid_f - mean
    square = jnp.sum(centred * centred, axis=1, keepdims=True)
    low = below_ref[half : half + 32, :].astype(F32)
    column_sum = low[:1] + low[8:9] + low[16:17]
    part_ref[:half, :] = (dot(resid, weight_ref[...]) - mean * column_sum).astype(BF16)
    stats = columns_of(split3(mean) + split3(square), half).T[:8]
    stats = jnp.concatenate([stats, jnp.zeros((8, hid - half), F32)], axis=1)
    part_ref[half : half + 32, :] = jnp.concatenate([low[:24], stats], axis=0).astype(BF16)


def write_copies(rows, copies_ref):
    for place in range(copies_ref.shape[0]):
        copies_ref[place] = rows


def total_of(y_ref):
    total = y_ref[0].astype(F32)
    for place in range(1, y_ref.shape[0]):
        total = total + y_ref[place].astype(F32)
    return total


def share_kernel(y_ref, resid_ref, bias_ref, copies_ref):
    rows = resid_ref[...] + total_of(y_ref) + bias_ref[...]
    write_copies(rows.astype(BF16), copies_ref)


def norm_kernel(y_ref, columns_ref, resid_ref, grad_ref, copies_ref):
    width = resid_ref.shape[1]
    summed = total_of(y_ref)
    grad_norm, extra = summed[:, :width], summed[:, width:] / D
    mean_grad = extra[:, :1] + extra[:, 1:2] + extra[:, 2:3]
    mean_cross = extra[:, 3:4] + extra[:, 4:5] + extra[:, 5:6]
    inv, mean = columns_ref[:, :1], columns_ref[:, 1:2]
    normed = (resid_ref[...] - mean) * inv
    grad_resid = inv * (grad_norm - mean_grad - normed * mean_cross)
    write_copies((grad_ref[...] + grad_resid).astype(BF16), copies_ref)


def effect_kernel(own_ref, rest_ref, resid_ref, weight_ref, bias_ref, *refs):
    outs, grads_ref = refs[:-1], refs[-1]
    half = own_ref.shape[0]
    core, place = lax.axis_index("section"), lax.axis_index("dp")
    grads_ref[pl.ds(pl.multiple_of(core * half, half), half), :] = own_ref[...]
    grads_ref[pl.ds(pl.multiple_of((1 - core) * half, half), half), :] = rest_ref[...]
    latents = weight_ref.shape[0]
    block = outs[0].shape[0]
    for by, out in enumerate(outs):
        start = pl.multiple_of(lax.rem(place + by, len(outs)) * block, block)
        grad = grads_ref[pl.ds(start, block), :]
        out[:, :latents] = dot_t(grad, weight_ref[...]).astype(BF16)
        resid = resid_ref[pl.ds(start, block), :].astype(F32)
        error = (resid - bias_ref[...]) * grad.astype(F32)
        error = jnp.sum(error, axis=1, keepdims=True) / lax.axis_size("latent")
        out[:, latents:] = columns_of(split3(error), block).astype(BF16)


def unpack_vectors(part, half):
    terms = part[..., half : half + 24, :].astype(F32)
    return terms[..., :8, :] + terms[..., 8:16, :] + terms[..., 16:24, :]


def on_device(
    tokens,
    cotangent,
    enc_weight,
    enc_bias,
    dec_weight,
    dec_bias,
    ln_gain,
    ln_bias,
    in_weight,
    in_bias,
    out_weight,
    out_bias,
):
    dp_count = lax.axis_size("dp")
    latent_count = lax.axis_size("latent")
    all_rows, width = tokens.shape
    half = all_rows // 2
    share = half // latent_count
    block = all_rows // dp_count
    hid = in_weight.shape[2]
    core = lax.axis_index("section")
    first = core == 0
    dp_place = lax.axis_index("dp")
    latent_place = lax.axis_index("latent")
    swap = [(0, 1), (1, 0)]

    def other(values):
        return lax.ppermute(values, "section", swap)

    def pick(mine_if_first, mine_if_second):
        return jnp.where(first, mine_if_first, mine_if_second)

    def own_rows(values):
        return lax.dynamic_slice_in_dim(values, latent_place * share, share, 0)

    in_w = in_weight[0]
    out_w = out_weight[0]

    def row_parts(resid):
        resid_f = resid.astype(F32)
        local_mean = jnp.mean(resid_f, axis=1)
        centred = resid_f - local_mean[:, None]
        return local_mean, jnp.sum(centred * centred, axis=1)

    def with_stats(part, local_mean, square):
        stats = jnp.stack(split3(local_mean) + split3(square))
        return part + jnp.pad(stats, ((half + 24, 2), (0, hid - half)))

    columns_shape = jax.ShapeDtypeStruct((half, 128), F32)
    y_shape = jax.ShapeDtypeStruct((half, width), BF16)
    grad_shape = jax.ShapeDtypeStruct((half, width + 128), BF16)
    flops = 2 * half * hid * width

    gained, mine, send = start_products(
        tokens, cotangent, in_w, out_w, ln_gain, ln_bias, in_bias, out_bias
    )
    there = other(send)
    tokens_half = lax.dynamic_slice_in_dim(tokens, core * half, half, 0)
    cot_half = lax.dynamic_slice_in_dim(cotangent, core * half, half, 0)
    part_0 = with_stats(pick(mine, there), *row_parts(tokens_half))
    part_grad = pick(there, mine)
    vectors_0 = unpack_vectors(part_0, half)
    vectors_1 = unpack_vectors(part_grad, half)
    gained_there = other(gained)
    gained_0, gained_1 = pick(gained, gained_there), pick(gained_there, gained)
    out_w0 = pick(out_w, other(out_w))

    y_0, state_0 = in_vmem(
        forward_kernel,
        (y_shape, jax.ShapeDtypeStruct((half + 8, hid + 128), F32)),
        *gather_ring(part_0, "dp"),
        out_w0,
        flops=flops,
    )
    tokens_rows = own_rows(tokens_half).astype(F32)
    bias_row = vectors_0[3:7].reshape(1, -1)[:, :width]
    row_shapes = (jax.ShapeDtypeStruct((latent_count, share, width), BF16),)
    (copies,) = in_vmem(
        share_kernel, row_shapes, exchange(y_0, "latent"), tokens_rows, bias_row
    )
    grad_act_1 = total_ring(part_grad[:half], "dp")
    copies, grad_act_1 = lax.optimization_barrier((copies, grad_act_1))
    resid_rows = copies[0]
    resid_half = lax.all_to_all(copies, "latent", 0, 0).reshape(half, width)

    (part_1,) = in_vmem(
        expand_kernel,
        (jax.ShapeDtypeStruct((half + 32, hid), BF16),),
        resid_half,
        gained_1,
        part_grad,
        flops=flops,
    )
    resid_there = other(resid_half)
    parts_1 = gather_ring(part_1, "dp")
    parts_1, resid_there = lax.optimization_barrier((parts_1, resid_there))

    def norm_grad(y, columns, resid, grad_rows):
        (copies,) = in_vmem(
            norm_kernel, row_shapes, exchange(y, "latent"), own_rows(columns), resid, grad_rows
        )
        return copies[0], lax.all_to_all(copies, "latent", 0, 0).reshape(half, width)

    y_1, columns_1 = in_vmem(
        turn_kernel, (grad_shape, columns_shape), *parts_1, grad_act_1, gained_1, flops=flops
    )
    cot_rows = own_rows(cot_half).astype(F32)
    grad_rows_1, grad_half_1 = norm_grad(y_1, columns_1, resid_rows.astype(F32), cot_rows)
    resid_all = pick(tokens, jnp.concatenate([resid_there, resid_half], axis=0))
    pre_codes = scatter_ring(dot(resid_all, enc_weight[0]).astype(BF16), "dp")
    grad_half_1, pre_codes = lax.optimization_barrier((grad_half_1, pre_codes))
    parts_0 = gather_ring(dot_t(grad_half_1, out_w0).astype(BF16), "dp")
    (y_2,) = in_vmem(
        backward_kernel, (grad_shape,), *parts_0, state_0, gained_0, flops=flops
    )
    _, grad_half_0 = norm_grad(y_2, state_0[:half, hid:], tokens_rows, grad_rows_1.astype(F32))

    codes = jnp.maximum(pre_codes + enc_bias[0][None], 0.0).astype(BF16)
    parts = in_vmem(
        effect_kernel,
        (jax.ShapeDtypeStruct((block, codes.shape[1] + 128), BF16),) * dp_count,
        pick(grad_half_0, grad_half_1),
        other(pick(grad_half_1, grad_half_0)),
        resid_all,
        dec_weight[0],
        dec_bias,
        flops=2 * all_rows * width * codes.shape[1],
        scratch=[pltpu.VMEM((all_rows, width), BF16)],
    )
    summed = parts[0].astype(F32) + sum(
        turn(parts[by], "dp", by).astype(F32) for by in range(1, dp_count)
    )
    latents = codes.shape[1]
    effect = codes.astype(F32) * summed[:, :latents]
    error = jnp.sum(summed[:, latents : latents + 3], axis=1) - jnp.sum(effect, axis=1)
    error = jnp.sum(spread(error[None], "latent"), axis=(0, 1))
    return effect.astype(BF16)[None], error[None]


def solution(mesh):
    in_specs = (
        P(None, "dp"),
        P(None, "dp"),
        P("section", "dp", "latent"),
        P("section", "latent"),
        P("section", "latent", "dp"),
        P("section", "dp"),
        P("section", "dp"),
        P("section", "dp"),
        P("section", "dp", "latent"),
        P("section", "latent"),
        P("section", "latent", "dp"),
        P("section", "dp"),
    )
    out_specs = (P("section", "dp", "latent"), P("section", "dp"))
    return jax.shard_map(
        on_device, mesh=mesh, in_specs=in_specs, out_specs=out_specs, check_vma=False
    )
```

```python
import jax
import jax.numpy as jnp
from jax import lax
from jax.experimental import pallas as pl
from jax.experimental.pallas import tpu as pltpu
from jax.sharding import PartitionSpec as P

D = 5120
EPSILON = 1e-05
SQRT_HALF = 0.7071067811865476
INV_SQRT_TAU = 0.3989422804014327
CONTRACT_LAST = (((1,), (1,)), ((), ()))
F32 = jnp.float32
BF16 = jnp.bfloat16


def gelu_slope(values):
    cumulative = 0.5 * (1.0 + lax.erf(values * SQRT_HALF))
    return cumulative + values * jnp.exp(-0.5 * values * values) * INV_SQRT_TAU


def split3(values):
    high = values.astype(BF16)
    rest = values - high.astype(F32)
    middle = rest.astype(BF16)
    low = (rest - middle.astype(F32)).astype(BF16)
    return [high, middle, low]


def dot(left, right):
    return jnp.dot(left, right, preferred_element_type=F32)


def dot_t(left, right):
    return lax.dot_general(left, right, CONTRACT_LAST, preferred_element_type=F32)


def spread(values, axis):
    count = lax.axis_size(axis)
    copies = jnp.broadcast_to(values[None], (count,) + values.shape)
    return lax.all_to_all(copies, axis, 0, 0)


def exchange(values, axis):
    count = lax.axis_size(axis)
    rows = values.shape[0] // count
    return lax.all_to_all(values.reshape(count, rows, values.shape[1]), axis, 0, 0)


def turn(values, axis, by):
    count = lax.axis_size(axis)
    return lax.ppermute(values, axis, [(i, (i + by) % count) for i in range(count)])


def gather_ring(values, axis):
    return [values] + [turn(values, axis, by) for by in range(1, lax.axis_size(axis))]


def total_ring(values, axis):
    return sum(part.astype(F32) for part in gather_ring(values, axis))


def scatter_ring(values, axis):
    count, place = lax.axis_size(axis), lax.axis_index(axis)
    rows = values.shape[0] // count

    def block(by):
        return lax.dynamic_slice_in_dim(values, (place + by) % count * rows, rows, 0)

    parts = [turn(block(by), axis, by) for by in range(1, count)]
    return block(0).astype(F32) + sum(part.astype(F32) for part in parts)


def start_kernel(
    tokens_hbm,
    cot_hbm,
    in_w_hbm,
    out_w_hbm,
    gain_hbm,
    bias_hbm,
    in_bias_hbm,
    out_bias_hbm,
    gained_ref,
    mine_ref,
    send_ref,
    tokens_ref,
    cot_ref,
    in_w_ref,
    out_w_ref,
    gain_ref,
    bias_ref,
    in_bias_ref,
    out_bias_ref,
    sems,
):
    width, hid = in_w_ref.shape
    half = tokens_ref.shape[0] // 2
    first = lax.axis_index("section") == 0
    pairs = (
        (gain_hbm, gain_ref),
        (in_w_hbm, in_w_ref),
        (bias_hbm, bias_ref),
        (in_bias_hbm, in_bias_ref),
        (out_bias_hbm, out_bias_ref),
        (tokens_hbm, tokens_ref),
        (cot_hbm, cot_ref),
        (out_w_hbm, out_w_ref),
    )
    copies = [pltpu.make_async_copy(a, b, sems.at[k]) for k, (a, b) in enumerate(pairs)]
    for copy in copies:
        copy.start()
    for copy in copies[:5]:
        copy.wait()
    gain = jnp.broadcast_to(gain_ref[...], (128, width)).T
    for at in range(0, hid, 128):
        columns = slice(at, at + 128)
        gained_ref[:, columns] = (in_w_ref[:, columns].astype(F32) * gain).astype(BF16)
    gained = gained_ref[...]
    column_sum = dot(jnp.ones((16, width), BF16), gained)[:1]
    terms = split3(bias_ref[...])
    terms = jnp.concatenate([t.astype(F32) for t in terms] + [jnp.zeros((13, width), F32)], axis=0)
    shift = jnp.sum(dot(terms.astype(BF16), in_w_ref[...]), axis=0, keepdims=True)
    rows = [column_sum, shift, in_bias_ref[...]]
    out_bias = out_bias_ref[...]
    for at in range(0, width, hid):
        piece = out_bias[:, at : at + hid]
        if piece.shape[1] < hid:
            piece = jnp.concatenate([piece, jnp.zeros((1, hid - piece.shape[1]), F32)], axis=1)
        rows.append(piece)
    rows.append(jnp.zeros((8 - len(rows), hid), F32))
    high = jnp.concatenate(rows, axis=0)
    packed = []
    for term in split3(high):
        packed.append(term.astype(F32))
    packed.append(jnp.zeros((8, hid), F32))
    packed = jnp.concatenate(packed, axis=0).astype(BF16)
    mine_ref[half : half + 32, :] = packed
    send_ref[half : half + 32, :] = packed

    for copy in copies[5:]:
        copy.wait()

    @pl.when(first)
    def _():
        for start, target in ((0, mine_ref), (half, send_ref)):
            rows = tokens_ref[start : start + half, :]
            mean = jnp.sum(rows.astype(F32), axis=1, keepdims=True) / width
            target[:half, :] = (dot(rows, gained) - mean * column_sum).astype(BF16)

    @pl.when(jnp.logical_not(first))
    def _():
        for start, target in ((half, mine_ref), (0, send_ref)):
            rows = cot_ref[start : start + half, :]
            target[:half, :] = dot_t(rows, out_w_ref[...]).astype(BF16)


def in_vmem(kernel, out_shape, *args, flops=0, scratch=()):
    return pl.pallas_call(
        kernel,
        out_shape=out_shape,
        in_specs=[pl.BlockSpec(memory_space=pltpu.VMEM)] * len(args),
        out_specs=tuple(pl.BlockSpec(memory_space=pltpu.VMEM) for _ in out_shape),
        scratch_shapes=scratch,
        compiler_params=pltpu.CompilerParams(vmem_limit_bytes=14 * 1024 * 1024),
        cost_estimate=pl.CostEstimate(flops=flops, bytes_accessed=4_000_000, transcendentals=0),
    )(*args)


def start_products(*args):
    tokens, _, in_w = args[:3]
    width, hid = in_w.shape
    half = tokens.shape[0] // 2
    part = jax.ShapeDtypeStruct((half + 32, hid), BF16)
    return pl.pallas_call(
        start_kernel,
        out_shape=(jax.ShapeDtypeStruct((width, hid), BF16), part, part),
        in_specs=[pl.BlockSpec(memory_space=pl.ANY)] * len(args),
        out_specs=(pl.BlockSpec(memory_space=pltpu.VMEM),) * 3,
        scratch_shapes=[pltpu.VMEM(arg.shape, arg.dtype) for arg in args]
        + [pltpu.SemaphoreType.DMA((len(args),))],
        compiler_params=pltpu.CompilerParams(vmem_limit_bytes=58 * 1024 * 1024),
        cost_estimate=pl.CostEstimate(
            flops=4 * half * width * hid, bytes_accessed=7_000_000, transcendentals=0
        ),
    )(*args)


def read_hidden(parts):
    half = parts[0].shape[0] - 32
    lower = [part[half : half + 32, :].astype(F32) for part in parts]
    vectors = [low[:8] + low[8:16] + low[16:24] for low in lower]
    means = [(low[24:25] + low[25:26] + low[26:27])[:, :half] for low in lower]
    squares = [(low[27:28] + low[28:29] + low[29:30])[:, :half] for low in lower]
    count = len(parts)
    mean = sum(means) / count
    aparts = [local_mean - mean for local_mean in means]
    variance = sum(squares) / D + sum(apart * apart for apart in aparts) / count
    rows = [lax.rsqrt(variance + EPSILON), mean] + aparts
    rows.append(jnp.zeros((128 - len(rows), half), F32))
    columns = jnp.concatenate(rows, axis=0).T
    total = parts[0][:half, :].astype(F32)
    for part in parts[1:]:
        total = total + part[:half, :].astype(F32)
    for place, vector in enumerate(vectors):
        total = total + columns[:, 2 + place : 3 + place] * vector[:1]
    pre = total * columns[:, :1]
    summed = sum(vectors)
    shift = summed[1:2] + vectors[0][2:3]
    return pre, shift, columns, summed


def forward_kernel(*refs):
    parts, (out_w_ref, y_ref, state_ref) = refs[:-3], refs[-3:]
    pre, shift, columns, sums = read_hidden(parts)
    hidden = pre + shift
    half, hid = pre.shape
    state_ref[:half, :hid] = pre
    state_ref[:half, hid:] = columns
    state_ref[half : half + 8, :hid] = jnp.concatenate([sums[:1], shift, sums[2:]], axis=0)
    act = 0.5 * hidden * (1.0 + lax.erf(hidden * SQRT_HALF))
    y_ref[...] = dot(act.astype(BF16), out_w_ref[...]).astype(BF16)


def write_grad(grad_act, hidden, pre, sums, weight, y_ref):
    width = weight.shape[0]
    grad_hidden = (grad_act * gelu_slope(hidden)).astype(BF16)
    grad_f = grad_hidden.astype(F32)
    total = jnp.sum(grad_f * sums, axis=1, keepdims=True)
    cross = jnp.sum(grad_f * pre, axis=1, keepdims=True)
    extra = columns_of(split3(total) + split3(cross), grad_f.shape[0])
    y_ref[:, :width] = dot_t(grad_hidden, weight).astype(BF16)
    y_ref[:, width:] = extra.astype(BF16)


def turn_kernel(*refs):
    parts, (grad_act_ref, weight_ref, y_ref, columns_ref) = refs[:-4], refs[-4:]
    pre, shift, columns, sums = read_hidden(parts)
    columns_ref[...] = columns
    write_grad(grad_act_ref[...], pre + shift, pre, sums[:1], weight_ref[...], y_ref)


def backward_kernel(*refs):
    parts, (state_ref, weight_ref, y_ref) = refs[:-3], refs[-3:]
    half, hid = parts[0].shape
    grad_act = parts[0][...].astype(F32)
    for part in parts[1:]:
        grad_act = grad_act + part[...].astype(F32)
    pre, vectors = state_ref[:half, :hid], state_ref[half : half + 8, :hid]
    write_grad(grad_act, pre + vectors[1:2], pre, vectors[:1], weight_ref[...], y_ref)


def columns_of(terms, rows):
    lane = lax.broadcasted_iota(jnp.int32, (rows, 128), 1)
    columns = jnp.zeros(lane.shape, F32)
    for index, term in enumerate(terms):
        columns = jnp.where(lane == index, term.astype(F32), columns)
    return columns


def expand_kernel(resid_ref, weight_ref, below_ref, part_ref):
    half, width = resid_ref.shape
    hid = weight_ref.shape[1]
    resid = resid_ref[...]
    resid_f = resid.astype(F32)
    mean = jnp.sum(resid_f, axis=1, keepdims=True) / width
    centred = resid_f - mean
    square = jnp.sum(centred * centred, axis=1, keepdims=True)
    low = below_ref[half : half + 32, :].astype(F32)
    column_sum = low[:1] + low[8:9] + low[16:17]
    part_ref[:half, :] = (dot(resid, weight_ref[...]) - mean * column_sum).astype(BF16)
    stats = columns_of(split3(mean) + split3(square), half).T[:8]
    stats = jnp.concatenate([stats, jnp.zeros((8, hid - half), F32)], axis=1)
    part_ref[half : half + 32, :] = jnp.concatenate([low[:24], stats], axis=0).astype(BF16)


def write_copies(rows, copies_ref):
    for place in range(copies_ref.shape[0]):
        copies_ref[place] = rows


def total_of(y_ref):
    total = y_ref[0].astype(F32)
    for place in range(1, y_ref.shape[0]):
        total = total + y_ref[place].astype(F32)
    return total


def share_kernel(y_ref, resid_ref, bias_ref, copies_ref):
    rows = resid_ref[...] + total_of(y_ref) + bias_ref[...]
    write_copies(rows.astype(BF16), copies_ref)


def norm_kernel(y_ref, columns_ref, resid_ref, grad_ref, copies_ref):
    width = resid_ref.shape[1]
    summed = total_of(y_ref)
    grad_norm, extra = summed[:, :width], summed[:, width:] / D
    mean_grad = extra[:, :1] + extra[:, 1:2] + extra[:, 2:3]
    mean_cross = extra[:, 3:4] + extra[:, 4:5] + extra[:, 5:6]
    inv, mean = columns_ref[:, :1], columns_ref[:, 1:2]
    normed = (resid_ref[...] - mean) * inv
    grad_resid = inv * (grad_norm - mean_grad - normed * mean_cross)
    write_copies((grad_ref[...] + grad_resid).astype(BF16), copies_ref)


def effect_kernel(own_ref, rest_ref, resid_ref, weight_ref, bias_ref, *refs):
    outs, grads_ref = refs[:-1], refs[-1]
    half = own_ref.shape[0]
    core, place = lax.axis_index("section"), lax.axis_index("dp")
    grads_ref[pl.ds(pl.multiple_of(core * half, half), half), :] = own_ref[...]
    grads_ref[pl.ds(pl.multiple_of((1 - core) * half, half), half), :] = rest_ref[...]
    latents = weight_ref.shape[0]
    block = outs[0].shape[0]
    for by, out in enumerate(outs):
        start = pl.multiple_of(lax.rem(place + by, len(outs)) * block, block)
        grad = grads_ref[pl.ds(start, block), :]
        out[:, :latents] = dot_t(grad, weight_ref[...]).astype(BF16)
        resid = resid_ref[pl.ds(start, block), :].astype(F32)
        error = (resid - bias_ref[...]) * grad.astype(F32)
        error = jnp.sum(error, axis=1, keepdims=True) / lax.axis_size("latent")
        out[:, latents:] = columns_of(split3(error), block).astype(BF16)


def unpack_vectors(part, half):
    terms = part[..., half : half + 24, :].astype(F32)
    return terms[..., :8, :] + terms[..., 8:16, :] + terms[..., 16:24, :]


def on_device(
    tokens,
    cotangent,
    enc_weight,
    enc_bias,
    dec_weight,
    dec_bias,
    ln_gain,
    ln_bias,
    in_weight,
    in_bias,
    out_weight,
    out_bias,
):
    dp_count = lax.axis_size("dp")
    latent_count = lax.axis_size("latent")
    all_rows, width = tokens.shape
    half = all_rows // 2
    share = half // latent_count
    block = all_rows // dp_count
    hid = in_weight.shape[2]
    core = lax.axis_index("section")
    first = core == 0
    dp_place = lax.axis_index("dp")
    latent_place = lax.axis_index("latent")
    swap = [(0, 1), (1, 0)]

    def other(values):
        return lax.ppermute(values, "section", swap)

    def pick(mine_if_first, mine_if_second):
        return jnp.where(first, mine_if_first, mine_if_second)

    def own_rows(values):
        return lax.dynamic_slice_in_dim(values, latent_place * share, share, 0)

    in_w = in_weight[0]
    out_w = out_weight[0]

    def row_parts(resid):
        resid_f = resid.astype(F32)
        local_mean = jnp.mean(resid_f, axis=1)
        centred = resid_f - local_mean[:, None]
        return local_mean, jnp.sum(centred * centred, axis=1)

    def with_stats(part, local_mean, square):
        stats = jnp.stack(split3(local_mean) + split3(square))
        return part + jnp.pad(stats, ((half + 24, 2), (0, hid - half)))

    columns_shape = jax.ShapeDtypeStruct((half, 128), F32)
    y_shape = jax.ShapeDtypeStruct((half, width), BF16)
    grad_shape = jax.ShapeDtypeStruct((half, width + 128), BF16)
    flops = 2 * half * hid * width

    gained, mine, send = start_products(
        tokens, cotangent, in_w, out_w, ln_gain, ln_bias, in_bias, out_bias
    )
    there = other(send)
    tokens_half = lax.dynamic_slice_in_dim(tokens, core * half, half, 0)
    cot_half = lax.dynamic_slice_in_dim(cotangent, core * half, half, 0)
    part_0 = with_stats(pick(mine, there), *row_parts(tokens_half))
    part_grad = pick(there, mine)
    vectors_0 = unpack_vectors(part_0, half)
    vectors_1 = unpack_vectors(part_grad, half)
    gained_there = other(gained)
    gained_0, gained_1 = pick(gained, gained_there), pick(gained_there, gained)
    out_w0 = pick(out_w, other(out_w))

    y_0, state_0 = in_vmem(
        forward_kernel,
        (y_shape, jax.ShapeDtypeStruct((half + 8, hid + 128), F32)),
        *gather_ring(part_0, "dp"),
        out_w0,
        flops=flops,
    )
    tokens_rows = own_rows(tokens_half).astype(F32)
    bias_row = vectors_0[3:7].reshape(1, -1)[:, :width]
    row_shapes = (jax.ShapeDtypeStruct((latent_count, share, width), BF16),)
    (copies,) = in_vmem(
        share_kernel, row_shapes, exchange(y_0, "latent"), tokens_rows, bias_row
    )
    grad_act_1 = total_ring(part_grad[:half], "dp")
    copies, grad_act_1 = lax.optimization_barrier((copies, grad_act_1))
    resid_rows = copies[0]
    resid_half = lax.all_to_all(copies, "latent", 0, 0).reshape(half, width)

    (part_1,) = in_vmem(
        expand_kernel,
        (jax.ShapeDtypeStruct((half + 32, hid), BF16),),
        resid_half,
        gained_1,
        part_grad,
        flops=flops,
    )
    resid_there = other(resid_half)
    parts_1 = gather_ring(part_1, "dp")
    parts_1, resid_there = lax.optimization_barrier((parts_1, resid_there))

    resid_all = pick(tokens, jnp.concatenate([resid_there, resid_half], axis=0))
    code_parts = dot(resid_all, enc_weight[0]).astype(BF16)

    def norm_grad(y, columns, resid, grad_rows, beside=None):
        y = exchange(y, "latent")
        if beside is not None:
            y, beside = lax.optimization_barrier((y, beside))
        (copies,) = in_vmem(norm_kernel, row_shapes, y, own_rows(columns), resid, grad_rows)
        return copies[0], beside, lax.all_to_all(copies, "latent", 0, 0).reshape(half, width)

    y_1, columns_1 = in_vmem(
        turn_kernel, (grad_shape, columns_shape), *parts_1, grad_act_1, gained_1, flops=flops
    )
    cot_rows = own_rows(cot_half).astype(F32)
    grad_rows_1, code_parts, grad_half_1 = norm_grad(
        y_1, columns_1, resid_rows.astype(F32), cot_rows, code_parts
    )
    pre_codes = scatter_ring(code_parts, "dp")
    grad_half_1, pre_codes = lax.optimization_barrier((grad_half_1, pre_codes))
    parts_0 = gather_ring(dot_t(grad_half_1, out_w0).astype(BF16), "dp")
    (y_2,) = in_vmem(
        backward_kernel, (grad_shape,), *parts_0, state_0, gained_0, flops=flops
    )
    _, _, grad_half_0 = norm_grad(y_2, state_0[:half, hid:], tokens_rows, grad_rows_1.astype(F32))

    codes = jnp.maximum(pre_codes + enc_bias[0][None], 0.0).astype(BF16)
    parts = in_vmem(
        effect_kernel,
        (jax.ShapeDtypeStruct((block, codes.shape[1] + 128), BF16),) * dp_count,
        pick(grad_half_0, grad_half_1),
        other(pick(grad_half_1, grad_half_0)),
        resid_all,
        dec_weight[0],
        dec_bias,
        flops=2 * all_rows * width * codes.shape[1],
        scratch=[pltpu.VMEM((all_rows, width), BF16)],
    )
    summed = parts[0].astype(F32) + sum(
        turn(parts[by], "dp", by).astype(F32) for by in range(1, dp_count)
    )
    latents = codes.shape[1]
    effect = codes.astype(F32) * summed[:, :latents]
    error = jnp.sum(summed[:, latents : latents + 3], axis=1) - jnp.sum(effect, axis=1)
    error = jnp.sum(spread(error[None], "latent"), axis=(0, 1))
    return effect.astype(BF16)[None], error[None]


def solution(mesh):
    in_specs = (
        P(None, "dp"),
        P(None, "dp"),
        P("section", "dp", "latent"),
        P("section", "latent"),
        P("section", "latent", "dp"),
        P("section", "dp"),
        P("section", "dp"),
        P("section", "dp"),
        P("section", "dp", "latent"),
        P("section", "latent"),
        P("section", "latent", "dp"),
        P("section", "dp"),
    )
    out_specs = (P("section", "dp", "latent"), P("section", "dp"))
    return jax.shard_map(
        on_device, mesh=mesh, in_specs=in_specs, out_specs=out_specs, check_vma=False
    )
```

```python
import jax
import jax.numpy as jnp
from jax import lax
from jax.experimental import pallas as pl
from jax.experimental.pallas import tpu as pltpu
from jax.sharding import PartitionSpec as P

D = 5120
EPSILON = 1e-05
SQRT_HALF = 0.7071067811865476
INV_SQRT_TAU = 0.3989422804014327
CONTRACT_LAST = (((1,), (1,)), ((), ()))
F32 = jnp.float32
BF16 = jnp.bfloat16


def gelu_slope(values):
    cumulative = 0.5 * (1.0 + lax.erf(values * SQRT_HALF))
    return cumulative + values * jnp.exp(-0.5 * values * values) * INV_SQRT_TAU


def split3(values):
    high = values.astype(BF16)
    rest = values - high.astype(F32)
    middle = rest.astype(BF16)
    low = (rest - middle.astype(F32)).astype(BF16)
    return [high, middle, low]


def dot(left, right):
    return jnp.dot(left, right, preferred_element_type=F32)


def dot_t(left, right):
    return lax.dot_general(left, right, CONTRACT_LAST, preferred_element_type=F32)


def spread(values, axis):
    count = lax.axis_size(axis)
    copies = jnp.broadcast_to(values[None], (count,) + values.shape)
    return lax.all_to_all(copies, axis, 0, 0)


def exchange(values, axis):
    count = lax.axis_size(axis)
    rows = values.shape[0] // count
    return lax.all_to_all(values.reshape(count, rows, values.shape[1]), axis, 0, 0)


def turn(values, axis, by):
    count = lax.axis_size(axis)
    return lax.ppermute(values, axis, [(i, (i + by) % count) for i in range(count)])


def gather_ring(values, axis):
    return [values] + [turn(values, axis, by) for by in range(1, lax.axis_size(axis))]


def total_ring(values, axis):
    return sum(part.astype(F32) for part in gather_ring(values, axis))


def scatter_ring(values, axis):
    count, place = lax.axis_size(axis), lax.axis_index(axis)
    rows = values.shape[0] // count

    def block(by):
        return lax.dynamic_slice_in_dim(values, (place + by) % count * rows, rows, 0)

    parts = [turn(block(by), axis, by) for by in range(1, count)]
    return block(0).astype(F32) + sum(part.astype(F32) for part in parts)


def start_kernel(
    tokens_hbm,
    cot_hbm,
    in_w_hbm,
    out_w_hbm,
    gain_hbm,
    bias_hbm,
    in_bias_hbm,
    out_bias_hbm,
    gained_ref,
    mine_ref,
    send_ref,
    tokens_ref,
    cot_ref,
    in_w_ref,
    out_w_ref,
    gain_ref,
    bias_ref,
    in_bias_ref,
    out_bias_ref,
    sems,
):
    width, hid = in_w_ref.shape
    half = tokens_ref.shape[0] // 2
    first = lax.axis_index("section") == 0
    pairs = (
        (gain_hbm, gain_ref),
        (in_w_hbm, in_w_ref),
        (bias_hbm, bias_ref),
        (in_bias_hbm, in_bias_ref),
        (out_bias_hbm, out_bias_ref),
        (tokens_hbm, tokens_ref),
        (cot_hbm, cot_ref),
        (out_w_hbm, out_w_ref),
    )
    copies = [pltpu.make_async_copy(a, b, sems.at[k]) for k, (a, b) in enumerate(pairs)]
    for copy in copies:
        copy.start()
    for copy in copies[:5]:
        copy.wait()
    gain = jnp.broadcast_to(gain_ref[...], (128, width)).T
    for at in range(0, hid, 128):
        columns = slice(at, at + 128)
        gained_ref[:, columns] = (in_w_ref[:, columns].astype(F32) * gain).astype(BF16)
    gained = gained_ref[...]
    column_sum = dot(jnp.ones((16, width), BF16), gained)[:1]
    terms = split3(bias_ref[...])
    terms = jnp.concatenate([t.astype(F32) for t in terms] + [jnp.zeros((13, width), F32)], axis=0)
    shift = jnp.sum(dot(terms.astype(BF16), in_w_ref[...]), axis=0, keepdims=True)
    rows = [column_sum, shift, in_bias_ref[...]]
    out_bias = out_bias_ref[...]
    for at in range(0, width, hid):
        piece = out_bias[:, at : at + hid]
        if piece.shape[1] < hid:
            piece = jnp.concatenate([piece, jnp.zeros((1, hid - piece.shape[1]), F32)], axis=1)
        rows.append(piece)
    rows.append(jnp.zeros((8 - len(rows), hid), F32))
    high = jnp.concatenate(rows, axis=0)
    packed = []
    for term in split3(high):
        packed.append(term.astype(F32))
    packed.append(jnp.zeros((8, hid), F32))
    packed = jnp.concatenate(packed, axis=0).astype(BF16)
    mine_ref[half : half + 32, :] = packed
    send_ref[half : half + 32, :] = packed

    for copy in copies[5:]:
        copy.wait()

    @pl.when(first)
    def _():
        for start, target in ((0, mine_ref), (half, send_ref)):
            rows = tokens_ref[start : start + half, :]
            mean = jnp.sum(rows.astype(F32), axis=1, keepdims=True) / width
            target[:half, :] = (dot(rows, gained) - mean * column_sum).astype(BF16)

    @pl.when(jnp.logical_not(first))
    def _():
        for start, target in ((half, mine_ref), (0, send_ref)):
            rows = cot_ref[start : start + half, :]
            target[:half, :] = dot_t(rows, out_w_ref[...]).astype(BF16)


def in_vmem(kernel, out_shape, *args, flops=0, scratch=()):
    return pl.pallas_call(
        kernel,
        out_shape=out_shape,
        in_specs=[pl.BlockSpec(memory_space=pltpu.VMEM)] * len(args),
        out_specs=tuple(pl.BlockSpec(memory_space=pltpu.VMEM) for _ in out_shape),
        scratch_shapes=scratch,
        compiler_params=pltpu.CompilerParams(vmem_limit_bytes=9 * 1024 * 1024),
        cost_estimate=pl.CostEstimate(flops=flops, bytes_accessed=4_000_000, transcendentals=0),
    )(*args)


def start_products(*args):
    tokens, _, in_w = args[:3]
    width, hid = in_w.shape
    half = tokens.shape[0] // 2
    part = jax.ShapeDtypeStruct((half + 32, hid), BF16)
    return pl.pallas_call(
        start_kernel,
        out_shape=(jax.ShapeDtypeStruct((width, hid), BF16), part, part),
        in_specs=[pl.BlockSpec(memory_space=pl.ANY)] * len(args),
        out_specs=(pl.BlockSpec(memory_space=pltpu.VMEM),) * 3,
        scratch_shapes=[pltpu.VMEM(arg.shape, arg.dtype) for arg in args]
        + [pltpu.SemaphoreType.DMA((len(args),))],
        compiler_params=pltpu.CompilerParams(vmem_limit_bytes=58 * 1024 * 1024),
        cost_estimate=pl.CostEstimate(
            flops=4 * half * width * hid, bytes_accessed=7_000_000, transcendentals=0
        ),
    )(*args)


def read_hidden(parts):
    half = parts[0].shape[0] - 32
    lower = [part[half : half + 32, :].astype(F32) for part in parts]
    vectors = [low[:8] + low[8:16] + low[16:24] for low in lower]
    means = [(low[24:25] + low[25:26] + low[26:27])[:, :half] for low in lower]
    squares = [(low[27:28] + low[28:29] + low[29:30])[:, :half] for low in lower]
    count = len(parts)
    mean = sum(means) / count
    aparts = [local_mean - mean for local_mean in means]
    variance = sum(squares) / D + sum(apart * apart for apart in aparts) / count
    rows = [lax.rsqrt(variance + EPSILON), mean] + aparts
    rows.append(jnp.zeros((128 - len(rows), half), F32))
    columns = jnp.concatenate(rows, axis=0).T
    total = parts[0][:half, :].astype(F32)
    for part in parts[1:]:
        total = total + part[:half, :].astype(F32)
    for place, vector in enumerate(vectors):
        total = total + columns[:, 2 + place : 3 + place] * vector[:1]
    pre = total * columns[:, :1]
    summed = sum(vectors)
    shift = summed[1:2] + vectors[0][2:3]
    return pre, shift, columns, summed


def forward_kernel(*refs):
    parts, (out_w_ref, y_ref, state_ref) = refs[:-3], refs[-3:]
    pre, shift, columns, sums = read_hidden(parts)
    hidden = pre + shift
    half, hid = pre.shape
    state_ref[:half, :hid] = pre
    state_ref[:half, hid:] = columns
    state_ref[half : half + 8, :hid] = jnp.concatenate([sums[:1], shift, sums[2:]], axis=0)
    act = 0.5 * hidden * (1.0 + lax.erf(hidden * SQRT_HALF))
    y_ref[...] = dot(act.astype(BF16), out_w_ref[...]).astype(BF16)


def write_grad(grad_act, hidden, pre, sums, weight, y_ref):
    width = weight.shape[0]
    grad_hidden = (grad_act * gelu_slope(hidden)).astype(BF16)
    grad_f = grad_hidden.astype(F32)
    total = jnp.sum(grad_f * sums, axis=1, keepdims=True)
    cross = jnp.sum(grad_f * pre, axis=1, keepdims=True)
    extra = columns_of(split3(total) + split3(cross), grad_f.shape[0])
    y_ref[:, :width] = dot_t(grad_hidden, weight).astype(BF16)
    y_ref[:, width:] = extra.astype(BF16)


def turn_kernel(*refs):
    parts, (grad_act_ref, weight_ref, y_ref, columns_ref) = refs[:-4], refs[-4:]
    pre, shift, columns, sums = read_hidden(parts)
    columns_ref[...] = columns
    write_grad(grad_act_ref[...], pre + shift, pre, sums[:1], weight_ref[...], y_ref)


def backward_kernel(*refs):
    parts, (state_ref, weight_ref, y_ref) = refs[:-3], refs[-3:]
    half, hid = parts[0].shape
    grad_act = parts[0][...].astype(F32)
    for part in parts[1:]:
        grad_act = grad_act + part[...].astype(F32)
    pre, vectors = state_ref[:half, :hid], state_ref[half : half + 8, :hid]
    write_grad(grad_act, pre + vectors[1:2], pre, vectors[:1], weight_ref[...], y_ref)


def columns_of(terms, rows):
    lane = lax.broadcasted_iota(jnp.int32, (rows, 128), 1)
    columns = jnp.zeros(lane.shape, F32)
    for index, term in enumerate(terms):
        columns = jnp.where(lane == index, term.astype(F32), columns)
    return columns


def expand_kernel(resid_ref, weight_ref, below_ref, part_ref):
    half, width = resid_ref.shape
    hid = weight_ref.shape[1]
    resid = resid_ref[...]
    resid_f = resid.astype(F32)
    mean = jnp.sum(resid_f, axis=1, keepdims=True) / width
    centred = resid_f - mean
    square = jnp.sum(centred * centred, axis=1, keepdims=True)
    low = below_ref[half : half + 32, :].astype(F32)
    column_sum = low[:1] + low[8:9] + low[16:17]
    part_ref[:half, :] = (dot(resid, weight_ref[...]) - mean * column_sum).astype(BF16)
    stats = columns_of(split3(mean) + split3(square), half).T[:8]
    stats = jnp.concatenate([stats, jnp.zeros((8, hid - half), F32)], axis=1)
    part_ref[half : half + 32, :] = jnp.concatenate([low[:24], stats], axis=0).astype(BF16)


def write_copies(rows, copies_ref):
    for place in range(copies_ref.shape[0]):
        copies_ref[place] = rows


def total_of(y_ref):
    total = y_ref[0].astype(F32)
    for place in range(1, y_ref.shape[0]):
        total = total + y_ref[place].astype(F32)
    return total


def share_kernel(y_ref, resid_ref, bias_ref, copies_ref):
    rows = resid_ref[...] + total_of(y_ref) + bias_ref[...]
    write_copies(rows.astype(BF16), copies_ref)


def norm_kernel(y_ref, columns_ref, resid_ref, grad_ref, copies_ref):
    width = resid_ref.shape[1]
    summed = total_of(y_ref)
    grad_norm, extra = summed[:, :width], summed[:, width:] / D
    mean_grad = extra[:, :1] + extra[:, 1:2] + extra[:, 2:3]
    mean_cross = extra[:, 3:4] + extra[:, 4:5] + extra[:, 5:6]
    inv, mean = columns_ref[:, :1], columns_ref[:, 1:2]
    normed = (resid_ref[...] - mean) * inv
    grad_resid = inv * (grad_norm - mean_grad - normed * mean_cross)
    write_copies((grad_ref[...] + grad_resid).astype(BF16), copies_ref)


def effect_kernel(own_ref, rest_ref, resid_ref, weight_ref, bias_ref, *refs):
    outs, grads_ref = refs[:-1], refs[-1]
    half = own_ref.shape[0]
    core, place = lax.axis_index("section"), lax.axis_index("dp")
    grads_ref[pl.ds(pl.multiple_of(core * half, half), half), :] = own_ref[...]
    grads_ref[pl.ds(pl.multiple_of((1 - core) * half, half), half), :] = rest_ref[...]
    latents = weight_ref.shape[0]
    block = outs[0].shape[0]
    for by, out in enumerate(outs):
        start = pl.multiple_of(lax.rem(place + by, len(outs)) * block, block)
        grad = grads_ref[pl.ds(start, block), :]
        out[:, :latents] = dot_t(grad, weight_ref[...]).astype(BF16)
        resid = resid_ref[pl.ds(start, block), :].astype(F32)
        error = (resid - bias_ref[...]) * grad.astype(F32)
        error = jnp.sum(error, axis=1, keepdims=True) / lax.axis_size("latent")
        out[:, latents:] = columns_of(split3(error), block).astype(BF16)


def unpack_vectors(part, half):
    terms = part[..., half : half + 24, :].astype(F32)
    return terms[..., :8, :] + terms[..., 8:16, :] + terms[..., 16:24, :]


def on_device(
    tokens,
    cotangent,
    enc_weight,
    enc_bias,
    dec_weight,
    dec_bias,
    ln_gain,
    ln_bias,
    in_weight,
    in_bias,
    out_weight,
    out_bias,
):
    dp_count = lax.axis_size("dp")
    latent_count = lax.axis_size("latent")
    all_rows, width = tokens.shape
    half = all_rows // 2
    share = half // latent_count
    block = all_rows // dp_count
    hid = in_weight.shape[2]
    core = lax.axis_index("section")
    first = core == 0
    dp_place = lax.axis_index("dp")
    latent_place = lax.axis_index("latent")
    swap = [(0, 1), (1, 0)]

    def other(values):
        return lax.ppermute(values, "section", swap)

    def pick(mine_if_first, mine_if_second):
        return jnp.where(first, mine_if_first, mine_if_second)

    def own_rows(values):
        return lax.dynamic_slice_in_dim(values, latent_place * share, share, 0)

    in_w = in_weight[0]
    out_w = out_weight[0]

    def row_parts(resid):
        resid_f = resid.astype(F32)
        local_mean = jnp.mean(resid_f, axis=1)
        centred = resid_f - local_mean[:, None]
        return local_mean, jnp.sum(centred * centred, axis=1)

    def with_stats(part, local_mean, square):
        stats = jnp.stack(split3(local_mean) + split3(square))
        return part + jnp.pad(stats, ((half + 24, 2), (0, hid - half)))

    columns_shape = jax.ShapeDtypeStruct((half, 128), F32)
    y_shape = jax.ShapeDtypeStruct((half, width), BF16)
    grad_shape = jax.ShapeDtypeStruct((half, width + 128), BF16)
    flops = 2 * half * hid * width

    gained, mine, send = start_products(
        tokens, cotangent, in_w, out_w, ln_gain, ln_bias, in_bias, out_bias
    )
    there = other(send)
    tokens_half = lax.dynamic_slice_in_dim(tokens, core * half, half, 0)
    cot_half = lax.dynamic_slice_in_dim(cotangent, core * half, half, 0)
    part_0 = with_stats(pick(mine, there), *row_parts(tokens_half))
    part_grad = pick(there, mine)
    vectors_0 = unpack_vectors(part_0, half)
    vectors_1 = unpack_vectors(part_grad, half)
    gained_there = other(gained)
    gained_0, gained_1 = pick(gained, gained_there), pick(gained_there, gained)
    out_w0 = pick(out_w, other(out_w))

    y_0, state_0 = in_vmem(
        forward_kernel,
        (y_shape, jax.ShapeDtypeStruct((half + 8, hid + 128), F32)),
        *gather_ring(part_0, "dp"),
        out_w0,
        flops=flops,
    )
    tokens_rows = own_rows(tokens_half).astype(F32)
    bias_row = vectors_0[3:7].reshape(1, -1)[:, :width]
    row_shapes = (jax.ShapeDtypeStruct((latent_count, share, width), BF16),)
    (copies,) = in_vmem(
        share_kernel, row_shapes, exchange(y_0, "latent"), tokens_rows, bias_row
    )
    grad_act_1 = total_ring(part_grad[:half], "dp")
    copies, grad_act_1 = lax.optimization_barrier((copies, grad_act_1))
    resid_rows = copies[0]
    resid_half = lax.all_to_all(copies, "latent", 0, 0).reshape(half, width)

    (part_1,) = in_vmem(
        expand_kernel,
        (jax.ShapeDtypeStruct((half + 32, hid), BF16),),
        resid_half,
        gained_1,
        part_grad,
        flops=flops,
    )
    resid_there = other(resid_half)
    parts_1 = gather_ring(part_1, "dp")
    parts_1, resid_there = lax.optimization_barrier((parts_1, resid_there))

    resid_all = pick(tokens, jnp.concatenate([resid_there, resid_half], axis=0))
    code_parts = dot(resid_all, enc_weight[0]).astype(BF16)

    def norm_grad(y, columns, resid, grad_rows, beside=None):
        y = exchange(y, "latent")
        if beside is not None:
            y, beside = lax.optimization_barrier((y, beside))
        (copies,) = in_vmem(norm_kernel, row_shapes, y, own_rows(columns), resid, grad_rows)
        return copies[0], beside, lax.all_to_all(copies, "latent", 0, 0).reshape(half, width)

    y_1, columns_1 = in_vmem(
        turn_kernel, (grad_shape, columns_shape), *parts_1, grad_act_1, gained_1, flops=flops
    )
    cot_rows = own_rows(cot_half).astype(F32)
    grad_rows_1, code_parts, grad_half_1 = norm_grad(
        y_1, columns_1, resid_rows.astype(F32), cot_rows, code_parts
    )
    pre_codes = scatter_ring(code_parts, "dp")
    grad_half_1, pre_codes = lax.optimization_barrier((grad_half_1, pre_codes))
    parts_0 = gather_ring(dot_t(grad_half_1, out_w0).astype(BF16), "dp")
    (y_2,) = in_vmem(
        backward_kernel, (grad_shape,), *parts_0, state_0, gained_0, flops=flops
    )
    _, _, grad_half_0 = norm_grad(y_2, state_0[:half, hid:], tokens_rows, grad_rows_1.astype(F32))

    codes = jnp.maximum(pre_codes + enc_bias[0][None], 0.0).astype(BF16)
    parts = in_vmem(
        effect_kernel,
        (jax.ShapeDtypeStruct((block, codes.shape[1] + 128), BF16),) * dp_count,
        pick(grad_half_0, grad_half_1),
        other(pick(grad_half_1, grad_half_0)),
        resid_all,
        dec_weight[0],
        dec_bias,
        flops=2 * all_rows * width * codes.shape[1],
        scratch=[pltpu.VMEM((all_rows, width), BF16)],
    )
    summed = parts[0].astype(F32) + sum(
        turn(parts[by], "dp", by).astype(F32) for by in range(1, dp_count)
    )
    latents = codes.shape[1]
    effect = codes.astype(F32) * summed[:, :latents]
    error = jnp.sum(summed[:, latents : latents + 3], axis=1) - jnp.sum(effect, axis=1)
    error = jnp.sum(spread(error[None], "latent"), axis=(0, 1))
    return effect.astype(BF16)[None], error[None]


def solution(mesh):
    in_specs = (
        P(None, "dp"),
        P(None, "dp"),
        P("section", "dp", "latent"),
        P("section", "latent"),
        P("section", "latent", "dp"),
        P("section", "dp"),
        P("section", "dp"),
        P("section", "dp"),
        P("section", "dp", "latent"),
        P("section", "latent"),
        P("section", "latent", "dp"),
        P("section", "dp"),
    )
    out_specs = (P("section", "dp", "latent"), P("section", "dp"))
    return jax.shard_map(
        on_device, mesh=mesh, in_specs=in_specs, out_specs=out_specs, check_vma=False
    )
```
